256 devices in a mesh: az: 128 (over z, x, y_hi, core), dep: 2 (over y_lo).
Axes of the slice: x: 4, y: 4 (y_hi: 2, y_lo: 2; y = y_hi * 2 + y_lo), z: 8, core: 2. Of those that a mesh axis runs over, the one named last changes fastest.
Arguments:
- field: float32 [8192, 2, 1024], P('az', None, 'dep'), may hold values from -6 to 6
- brick_speed: bfloat16 [32768, 1024], P('az', 'dep'), may hold values from -40 to 40
- send_index: int32 [128, 128, 32], P('az'), may hold values from 0 to 255
- send_count: int32 [128, 128], P('az'), may hold values from 0 to 32, as said below
- weights: bfloat16 [8192, 4, 4096], P('az'), may hold values from 0 to 1, as said below
- propagator: bfloat16 [2, 2, 1024, 1024], replicated, may hold values from -1 to 1
Outputs:
- pressure: float32 [8192, 2, 1024], P('az', None, 'dep')
The draws below stay inside these ranges and needn't reach their ends.
Inputs may be any that keep to these rules, and one draw needn't show every extreme that they name: `send_count`: 32 or fewer columns from one brick to one sector; one sector receives 32 from every brick. Nonnegative interpolation weights.
All inputs are finite; a program needn't handle non-finite values.
Results may differ from the reference program's by a relative error of at most 0.025.
Values may be sent and summed in bfloat16 or wider, within the bound.
No kernel may reach another device: no remote copies, remote signals or barrier semaphores. Data moves between devices by JAX's collectives and lax.ppermute only.
A program may use at most 64 MiB of HBM per device.

```python
import jax
import jax.numpy as jnp
from jax import lax

NZ = 1024
AZ_DEV = 64
BCOL = 256
CAP = 32
NSTEP = 4
NPADE = 2
SECTORS = 128
AZ = 8192


def intersection_counts(key):
    inner = jax.random.fold_in(key, 11)
    first, second = jax.random.split(inner)
    base = jax.random.randint(first, (SECTORS, SECTORS), 0, CAP + 1)
    busiest = jax.random.randint(second, (), 0, SECTORS)
    column = lax.broadcasted_iota(jnp.int32, (SECTORS, SECTORS), 1)
    return jnp.where(column == busiest, CAP, base).astype(jnp.int32)


def draw_send_count(key, part):
    return intersection_counts(key)


def draw_weights(key, part):
    inner = jax.random.fold_in(key, 23)
    first, second = jax.random.split(inner)
    picked = jax.random.randint(first, (AZ, NSTEP, SECTORS * CAP), 0, SECTORS * CAP) < 32
    values = jax.random.uniform(second, (AZ, NSTEP, SECTORS * CAP), jnp.float32, 0.03, 0.1)
    return jnp.where(picked, values, 0.0).astype(jnp.bfloat16)


def draw_propagator(key, part):
    inner = jax.random.fold_in(key, 37)
    first, second = jax.random.split(inner)
    phase = jax.random.uniform(first, (NPADE, NZ), jnp.float32, -jnp.pi, jnp.pi)
    noise = jax.random.truncated_normal(second, -3.0, 3.0, (NPADE, 2, NZ, NZ), jnp.float32)
    noise = noise * (0.5 / NZ ** 0.5)
    rowid = lax.broadcasted_iota(jnp.int32, (NZ, NZ), 0)
    colid = lax.broadcasted_iota(jnp.int32, (NZ, NZ), 1)
    identity = (rowid == colid).astype(jnp.float32)
    diag_real = jnp.cos(phase)[:, :, None] * identity[None]
    diag_imag = jnp.sin(phase)[:, :, None] * identity[None]
    matrix = jnp.stack([diag_real, diag_imag], axis=1) + noise
    return (matrix / 1.5 ** 0.5).astype(jnp.bfloat16)


def touch_ends(values, own_key, least, largest):
    shape = values.shape
    spot = [jax.random.randint(jax.random.fold_in(own_key, axis), (), 0, shape[axis]) for axis in range(len(shape))]
    values = values.at[tuple(spot)].set(least)
    longest = shape.index(max(shape))
    spot[longest] = (spot[longest] + 1) % shape[longest]
    return values.at[tuple(spot)].set(largest)


def steps_of(own_key, shape, cuts, least, largest):
    gain = 1.0
    for dim, blocks in cuts:
        steps = jax.random.uniform(jax.random.fold_in(jax.random.fold_in(own_key, 6), dim), (blocks,), jnp.float32, least / len(cuts), largest / len(cuts))
        gain = gain * jnp.repeat(jnp.exp(steps), shape[dim] // blocks).reshape((-1,) + (1,) * (len(shape) - 1 - dim))
    return gain


def gaussian(stream_key, shape, scale, bound, pieces=(), kind=jnp.bfloat16):
    gain = steps_of(stream_key, shape, pieces, -0.22, 0.18) if pieces else 1.0
    drawn = jax.random.normal(stream_key, shape, jnp.float32) * scale * gain
    return jnp.minimum(jnp.maximum(drawn, -bound), bound).astype(kind)


def setup_inputs(seed: int = 0) -> dict:
    keys = jax.random.split(jax.random.key(seed), 7)
    field = gaussian(keys[0], (AZ, 2, NZ), 1.0, 6.0, ((0, 128), (2, 2)), jnp.float32)
    brick_speed = jnp.clip(jax.random.uniform(keys[1], (SECTORS * BCOL, NZ), jnp.float32, -40.0, 40.0) * steps_of(keys[1], (SECTORS * BCOL, NZ), ((0, 128), (1, 2)), -0.4, 0.0), -40.0, 40.0).astype(jnp.bfloat16)
    send_index = touch_ends(jax.random.randint(keys[2], (SECTORS, SECTORS, CAP), 0, BCOL), jax.random.fold_in(keys[2], 1), 0, BCOL - 1).astype(jnp.int32)
    send_count = draw_send_count(jax.random.fold_in(keys[6], 71), 0)
    weights = draw_weights(jax.random.fold_in(keys[6], 71), 0)
    propagator = draw_propagator(jax.random.fold_in(keys[6], 71), 0)
    return dict(field=field, brick_speed=brick_speed, send_index=send_index, send_count=send_count, weights=weights, propagator=propagator)


angle_rate = 200.0 / 1500.0
couple_real = 0.1
couple_imag = 0.15


def apply_screen(field, angle):
    cosine = jnp.cos(angle)
    sine = jnp.sin(angle)
    real_part = field[:, 0] * cosine - field[:, 1] * sine
    imag_part = field[:, 0] * sine + field[:, 1] * cosine
    return jnp.stack([real_part, imag_part], axis=1)


def azimuth_couple(padded, rows):
    laplace = (-padded[0:rows] + 16.0 * padded[1:rows + 1] - 30.0 * padded[2:rows + 2]
               + 16.0 * padded[3:rows + 3] - padded[4:rows + 4]) / 12.0
    centre = padded[2:rows + 2]
    real_part = centre[:, 0] + couple_real * laplace[:, 0] - couple_imag * laplace[:, 1]
    imag_part = centre[:, 1] + couple_real * laplace[:, 1] + couple_imag * laplace[:, 0]
    return jnp.stack([real_part, imag_part], axis=1)


def combine_parts(mixed):
    real_part = mixed[:, 0, 0] - mixed[:, 1, 1]
    imag_part = mixed[:, 0, 1] + mixed[:, 1, 0]
    return jnp.stack([real_part, imag_part], axis=1)


def reference(field, brick_speed, send_index, send_count, weights, propagator):
    offsets = (jnp.arange(SECTORS, dtype=jnp.int32) * BCOL)[:, None]

    def one_sector(sector):
        chosen = lax.dynamic_index_in_dim(send_index, sector, 1, keepdims=False)
        limit = lax.dynamic_index_in_dim(send_count, sector, 1, keepdims=False)
        received = brick_speed[chosen + offsets]
        slots = lax.broadcasted_iota(jnp.int32, chosen.shape, 1)
        keep = (slots < limit[:, None])[:, :, None]
        received = jnp.where(keep, received, jnp.zeros_like(received))
        block = lax.dynamic_slice_in_dim(weights, sector * AZ_DEV, AZ_DEV, 0)
        flat = received.reshape(SECTORS * CAP, NZ)
        return jnp.einsum('akm,mz->akz', block.astype(jnp.float32), flat.astype(jnp.float32))

    speed = lax.map(one_sector, jnp.arange(SECTORS, dtype=jnp.int32)).reshape(AZ, NSTEP, NZ)
    angle = -angle_rate * speed
    for step in range(NSTEP):
        field = apply_screen(field, angle[:, step, :])
        padded = jnp.concatenate([field[-2:], field, field[:2]], axis=0)
        field = azimuth_couple(padded, AZ)
        for factor in range(NPADE):
            rounded = lax.optimization_barrier(field.astype(jnp.bfloat16))
            mixed = jnp.einsum('acz,pzw->acpw', rounded.astype(jnp.float32),
                               propagator[factor].astype(jnp.float32))
            field = combine_parts(mixed)
    return field
```

```python
import math

import jax
import jax.numpy as jnp
from jax import lax
from jax.experimental import pallas as pl
from jax.experimental.pallas import tpu as pltpu
from jax.sharding import Mesh, PartitionSpec as P

angle_rate = 200.0 / 1500.0
couple_real = 0.1
couple_imag = 0.15

AXES = ("z", "x", "yh", "c", "yl")
SECTOR = ("z", "x", "yh", "c")
SIZES = (8, 4, 2, 2, 2)
HALO = 8
ROWS = 32
EXT = ROWS + 2 * HALO
NZ = 1024
STEPS = 4
FACTORS = 2
RING = 256


def encode_turns(speed):
    turns = speed * (-angle_rate / (2.0 * math.pi))
    code = jnp.round((turns - jnp.round(turns)) * 65536.0).astype(jnp.int32)
    return jnp.where(code > 32767, -32768, code).astype(jnp.int16)


def cos_sin(code):
    quadrant = (code + 8192) >> 14
    part = (code - (quadrant << 14)).astype(jnp.float32) * (1.0 / 16384.0)
    square = part * part
    h = math.pi / 2
    sine = part * (h + square * (-(h**3) / 6 + square * (h**5 / 120 - square * (h**7 / 5040))))
    cosine = 1.0 + square * (
        -(h**2) / 2 + square * (h**4 / 24 + square * (-(h**6) / 720 + square * (h**8 / 40320)))
    )
    odd = (quadrant & 1) == 1
    first = jnp.where(odd, sine, cosine)
    second = jnp.where(odd, cosine, sine)
    first = jnp.where(((quadrant + 1) & 2) == 2, -first, first)
    second = jnp.where((quadrant & 2) == 2, -second, second)
    return first, second


def march_kernel(
    side, code, code_left, code_right, field, field_left, field_right, factors, keep, send, state, padded, rounded
):
    state[:, 0:HALO] = field_left[...]
    state[:, HALO : HALO + ROWS] = field[...]
    state[:, HALO + ROWS : EXT] = field_right[...]
    padded[:, 0:HALO] = jnp.zeros((2, HALO, NZ), jnp.float32)
    padded[:, HALO + EXT :] = jnp.zeros((2, HALO, NZ), jnp.float32)
    pieces = ((code_left, HALO, 0), (code, ROWS, HALO), (code_right, HALO, HALO + ROWS))
    for step in range(STEPS):
        for ref, rows, start in pieces:
            value = ref[step * rows : (step + 1) * rows, :] if rows == ROWS else ref[...][step * rows : (step + 1) * rows, :]
            cosine, sine = cos_sin(value.astype(jnp.int32))
            real = state[0, start : start + rows]
            imag = state[1, start : start + rows]
            padded[0, HALO + start : HALO + start + rows] = real * cosine - imag * sine
            padded[1, HALO + start : HALO + start + rows] = real * sine + imag * cosine
        laplace = []
        for part in range(2):
            near = padded[part, HALO - 1 : HALO - 1 + EXT] + padded[part, HALO + 1 : HALO + 1 + EXT]
            far = padded[part, HALO - 2 : HALO - 2 + EXT] + padded[part, HALO + 2 : HALO + 2 + EXT]
            centre = padded[part, HALO : HALO + EXT]
            laplace.append((16.0 * near - far - 30.0 * centre) * (1.0 / 12.0))
        rounded[0:EXT] = (
            padded[0, HALO : HALO + EXT] + couple_real * laplace[0] - couple_imag * laplace[1]
        ).astype(jnp.bfloat16)
        rounded[EXT : 2 * EXT] = (
            padded[1, HALO : HALO + EXT] + couple_real * laplace[1] + couple_imag * laplace[0]
        ).astype(jnp.bfloat16)
        for factor in range(FACTORS):
            left = rounded[...]
            for column in range(0, NZ, 256):
                by_real = jnp.dot(
                    left, factors[factor, 0, :, column : column + 256], preferred_element_type=jnp.float32
                )
                by_imag = jnp.dot(
                    left, factors[factor, 1, :, column : column + 256], preferred_element_type=jnp.float32
                )
                state[0, :, column : column + 256] = by_real[:EXT] - by_imag[EXT:]
                state[1, :, column : column + 256] = by_imag[:EXT] + by_real[EXT:]
            if factor + 1 < FACTORS:
                rounded[0:EXT] = state[0].astype(jnp.bfloat16)
                rounded[EXT : 2 * EXT] = state[1].astype(jnp.bfloat16)
    low = state[:, HALO : HALO + ROWS, 0 : NZ // 2]
    high = state[:, HALO : HALO + ROWS, NZ // 2 :]
    first = side[0] == 0
    keep[...] = jnp.where(first, low, high)
    send[...] = jnp.where(first, high, low).astype(jnp.bfloat16)


def march(side, code, code_left, code_right, field, field_left, field_right, factors):
    half = (2, ROWS, NZ // 2)
    vmem = pl.BlockSpec(memory_space=pltpu.VMEM)
    return pl.pallas_call(
        march_kernel,
        out_shape=(jax.ShapeDtypeStruct(half, jnp.float32), jax.ShapeDtypeStruct(half, jnp.bfloat16)),
        in_specs=[pl.BlockSpec(memory_space=pltpu.SMEM)] + [vmem] * 7,
        out_specs=(vmem, vmem),
        scratch_shapes=[
            pltpu.VMEM((2, EXT, NZ), jnp.float32),
            pltpu.VMEM((2, EXT + 2 * HALO, NZ), jnp.float32),
            pltpu.VMEM((2 * EXT, NZ), jnp.bfloat16),
        ],
        compiler_params=pltpu.CompilerParams(vmem_limit_bytes=24 * 1024 * 1024),
        cost_estimate=pl.CostEstimate(
            flops=2 * 8 * 2 * EXT * NZ * 2 * NZ, bytes_accessed=10 * 1024 * 1024, transcendentals=0
        ),
        name="march",
    )(side, code, code_left, code_right, field, field_left, field_right, factors)


def swap_dep(value):
    return lax.ppermute(value, "yl", [(0, 1), (1, 0)])


def ring_step(value, shift):
    return lax.ppermute(value, AXES, [(i, (i + shift) % RING) for i in range(RING)])


def own_rows_all_depths(first, value, dim, depth_dim):
    top = lax.slice_in_dim(value, 0, ROWS, axis=dim)
    bottom = lax.slice_in_dim(value, ROWS, 2 * ROWS, axis=dim)
    mine = jnp.where(first, top, bottom)
    other = swap_dep(jnp.where(first, bottom, top))
    return jnp.where(
        first, jnp.concatenate([mine, other], depth_dim), jnp.concatenate([other, mine], depth_dim)
    )


def with_halo(value):
    before = ring_step(value[:, ROWS - HALO :], 1)
    after = ring_step(value[:, :HALO], -1)
    return before, after


def per_device(field, brick_speed, send_index, send_count, weights, propagator):
    first = lax.axis_index("yl") == 0
    chosen = send_index[0]
    limit = send_count[0]
    slots = lax.broadcasted_iota(jnp.int32, chosen.shape, 1)
    chosen = jnp.where(slots < limit[:, None], chosen, -1)
    columns = lax.broadcasted_iota(jnp.int32, chosen.shape + (brick_speed.shape[0],), 2)
    onehot = (chosen[:, :, None] == columns).astype(jnp.bfloat16)
    packed = jnp.einsum("dmc,cz->dmz", onehot, brick_speed, preferred_element_type=jnp.float32).astype(jnp.bfloat16)
    piece = lax.all_to_all(packed, SECTOR, split_axis=0, concat_axis=0, tiled=True)
    flat = piece.reshape(piece.shape[0] * piece.shape[1], piece.shape[2])

    own = own_rows_all_depths(first, field.transpose(1, 0, 2), 1, 2)
    own_left, own_right = with_halo(own)

    speed = jnp.einsum("akm,mz->kaz", weights, flat, preferred_element_type=jnp.float32)
    code = own_rows_all_depths(first, encode_turns(speed), 1, 2)
    code_left, code_right = with_halo(code)

    side = jnp.where(first, 0, 1).astype(jnp.int32).reshape(1)
    keep, send = march(
        side,
        code.reshape(STEPS * ROWS, NZ),
        code_left.reshape(STEPS * HALO, NZ),
        code_right.reshape(STEPS * HALO, NZ),
        own,
        own_left,
        own_right,
        propagator,
    )
    other = swap_dep(send).astype(jnp.float32)
    out = jnp.where(first, jnp.concatenate([keep, other], 1), jnp.concatenate([other, keep], 1))
    return out.transpose(1, 0, 2)


def solution(mesh):
    inner = Mesh(mesh.devices.reshape(SIZES), AXES)
    placed = (
        P(SECTOR, None, "yl"),
        P(SECTOR, "yl"),
        P(SECTOR, None, None),
        P(SECTOR, None),
        P(SECTOR, None, None),
        P(),
    )
    return jax.shard_map(
        per_device, mesh=inner, in_specs=placed, out_specs=P(SECTOR, None, "yl"), check_vma=False
    )
```

```python
import math

import jax
import jax.numpy as jnp
from jax import lax
from jax.experimental import pallas as pl
from jax.experimental.pallas import tpu as pltpu
from jax.sharding import Mesh, PartitionSpec as P

angle_rate = 200.0 / 1500.0
couple_real = 0.1
couple_imag = 0.15

AXES = ("z", "x", "yh", "c", "yl")
SECTOR = ("z", "x", "yh", "c")
SIZES = (8, 4, 2, 2, 2)
HALO = 8
ROWS = 32
EXT = ROWS + 2 * HALO
NZ = 1024
STEPS = 4
FACTORS = 2
RING = 256


def turn_code(speed):
    turns = speed * (-angle_rate / (2.0 * math.pi))
    code = jnp.round((turns - jnp.round(turns)) * 65536.0).astype(jnp.int32)
    return jnp.where(code > 32767, -32768, code)


def cos_sin(code):
    quadrant = (code + 8192) >> 14
    part = (code - (quadrant << 14)).astype(jnp.float32) * (1.0 / 16384.0)
    square = part * part
    h = math.pi / 2
    sine = part * (h + square * (-(h**3) / 6 + square * (h**5 / 120 - square * (h**7 / 5040))))
    cosine = 1.0 + square * (
        -(h**2) / 2 + square * (h**4 / 24 + square * (-(h**6) / 720 + square * (h**8 / 40320)))
    )
    odd = (quadrant & 1) == 1
    first = jnp.where(odd, sine, cosine)
    second = jnp.where(odd, cosine, sine)
    first = jnp.where(((quadrant + 1) & 2) == 2, -first, first)
    second = jnp.where((quadrant & 2) == 2, -second, second)
    return first, second


def march_kernel(
    side, code, code_left, code_right, field, field_left, field_right, factors, keep, send, state, padded, rounded
):
    state[:, 0:HALO] = field_left[...]
    state[:, HALO : HALO + ROWS] = field[...]
    state[:, HALO + ROWS : EXT] = field_right[...]
    padded[:, 0:HALO] = jnp.zeros((2, HALO, NZ), jnp.float32)
    padded[:, HALO + EXT :] = jnp.zeros((2, HALO, NZ), jnp.float32)
    pieces = ((code_left, HALO, 0), (code, ROWS, HALO), (code_right, HALO, HALO + ROWS))
    for step in range(STEPS):
        for ref, rows, start in pieces:
            value = ref[step * rows : (step + 1) * rows, :] if rows == ROWS else ref[...][step * rows : (step + 1) * rows, :]
            cosine, sine = cos_sin(value.astype(jnp.int32))
            real = state[0, start : start + rows]
            imag = state[1, start : start + rows]
            padded[0, HALO + start : HALO + start + rows] = real * cosine - imag * sine
            padded[1, HALO + start : HALO + start + rows] = real * sine + imag * cosine
        laplace = []
        for part in range(2):
            near = padded[part, HALO - 1 : HALO - 1 + EXT] + padded[part, HALO + 1 : HALO + 1 + EXT]
            far = padded[part, HALO - 2 : HALO - 2 + EXT] + padded[part, HALO + 2 : HALO + 2 + EXT]
            centre = padded[part, HALO : HALO + EXT]
            laplace.append((16.0 * near - far - 30.0 * centre) * (1.0 / 12.0))
        rounded[0:EXT] = (
            padded[0, HALO : HALO + EXT] + couple_real * laplace[0] - couple_imag * laplace[1]
        ).astype(jnp.bfloat16)
        rounded[EXT : 2 * EXT] = (
            padded[1, HALO : HALO + EXT] + couple_real * laplace[1] + couple_imag * laplace[0]
        ).astype(jnp.bfloat16)
        for factor in range(FACTORS):
            left = rounded[...]
            for column in range(0, NZ, 256):
                by_real = jnp.dot(
                    left, factors[factor, 0, :, column : column + 256], preferred_element_type=jnp.float32
                )
                by_imag = jnp.dot(
                    left, factors[factor, 1, :, column : column + 256], preferred_element_type=jnp.float32
                )
                state[0, :, column : column + 256] = by_real[:EXT] - by_imag[EXT:]
                state[1, :, column : column + 256] = by_imag[:EXT] + by_real[EXT:]
            if factor + 1 < FACTORS:
                rounded[0:EXT] = state[0].astype(jnp.bfloat16)
                rounded[EXT : 2 * EXT] = state[1].astype(jnp.bfloat16)
    low = state[:, HALO : HALO + ROWS, 0 : NZ // 2]
    high = state[:, HALO : HALO + ROWS, NZ // 2 :]
    first = side[0] == 0
    keep[...] = jnp.where(first, low, high)
    send[...] = jnp.where(first, high, low).astype(jnp.bfloat16)


def march(side, code, code_left, code_right, field, field_left, field_right, factors):
    half = (2, ROWS, NZ // 2)
    vmem = pl.BlockSpec(memory_space=pltpu.VMEM)
    return pl.pallas_call(
        march_kernel,
        out_shape=(jax.ShapeDtypeStruct(half, jnp.float32), jax.ShapeDtypeStruct(half, jnp.bfloat16)),
        in_specs=[pl.BlockSpec(memory_space=pltpu.SMEM)] + [vmem] * 7,
        out_specs=(vmem, vmem),
        scratch_shapes=[
            pltpu.VMEM((2, EXT, NZ), jnp.float32),
            pltpu.VMEM((2, EXT + 2 * HALO, NZ), jnp.float32),
            pltpu.VMEM((2 * EXT, NZ), jnp.bfloat16),
        ],
        compiler_params=pltpu.CompilerParams(vmem_limit_bytes=24 * 1024 * 1024),
        cost_estimate=pl.CostEstimate(
            flops=2 * 8 * 2 * EXT * NZ * 2 * NZ, bytes_accessed=10 * 1024 * 1024, transcendentals=0
        ),
        name="march",
    )(side, code, code_left, code_right, field, field_left, field_right, factors)


def swap_dep(value):
    return lax.ppermute(value, "yl", [(0, 1), (1, 0)])


def ring_step(value, shift):
    return lax.ppermute(value, AXES, [(i, (i + shift) % RING) for i in range(RING)])


def own_rows_all_depths(first, value, dim, depth_dim):
    top = lax.slice_in_dim(value, 0, ROWS, axis=dim)
    bottom = lax.slice_in_dim(value, ROWS, 2 * ROWS, axis=dim)
    mine = jnp.where(first, top, bottom)
    other = swap_dep(jnp.where(first, bottom, top))
    return jnp.where(
        first, jnp.concatenate([mine, other], depth_dim), jnp.concatenate([other, mine], depth_dim)
    )


def with_halo(value):
    before = ring_step(value[:, ROWS - HALO :], 1)
    after = ring_step(value[:, :HALO], -1)
    return before, after


PLANE = 8
SLOTS = 512
BCOL = 256
CAP = 32
DEPTH = NZ // 2


def pack_kernel(place, *refs):
    count = 2 * len(SHIFTS)
    pieces = refs[: 2 * count]
    weights, out, packed = refs[2 * count :]
    z, core = place[0], place[1]
    line = lax.broadcasted_iota(jnp.int32, (16, BCOL), 0)
    column = lax.broadcasted_iota(jnp.int32, (BCOL // 2, BCOL), 0)
    for brick in range(count):
        low, high = pieces[2 * brick], pieces[2 * brick + 1]
        index = low[BCOL // 2 :, 0:BCOL].astype(jnp.float32)
        index = jnp.sum(jnp.where(line == z * 2 + core, index, 0.0), axis=0, keepdims=True).astype(jnp.int32)
        total = None
        for half, ref in enumerate((low, high)):
            onehot = jnp.where(column + half * (BCOL // 2) == index, 1.0, 0.0).astype(jnp.bfloat16)
            part = lax.dot_general(
                onehot, ref[0 : BCOL // 2, :], (((0,), (0,)), ((), ())), preferred_element_type=jnp.float32
            )
            total = part if total is None else total + part
        from_z = lax.rem(z + SHIFTS[brick % len(SHIFTS)] + 8, 8)
        from_core = core if brick < len(SHIFTS) else 1 - core
        start = pl.multiple_of((from_z * 2 + from_core) * CAP, CAP)
        packed[:, pl.ds(start, CAP), :] = total.astype(jnp.bfloat16).reshape(PLANE, CAP, DEPTH)
    for sector in range(PLANE):
        code = turn_code(
            jnp.dot(weights[sector], packed[sector], preferred_element_type=jnp.float32)
        ).astype(jnp.int16)
        for step in range(STEPS):
            for side in range(2):
                start = step * 2 * ROWS + side * ROWS
                out[sector, side, step * ROWS : (step + 1) * ROWS, :] = code[start : start + ROWS]


SHIFTS = (0, -1, 1, -2, 2, -3, 3, 4)


def pack(place, pieces, weights):
    vmem = pl.BlockSpec(memory_space=pltpu.VMEM)
    return pl.pallas_call(
        pack_kernel,
        out_shape=jax.ShapeDtypeStruct((PLANE, 2, STEPS * ROWS, DEPTH), jnp.int16),
        in_specs=[pl.BlockSpec(memory_space=pltpu.SMEM)] + [vmem] * (len(pieces) + 1),
        out_specs=vmem,
        scratch_shapes=[pltpu.VMEM((PLANE, SLOTS, DEPTH), jnp.bfloat16)],
        compiler_params=pltpu.CompilerParams(vmem_limit_bytes=28 * 1024 * 1024),
        cost_estimate=pl.CostEstimate(flops=4 * 537_000_000, bytes_accessed=8 * 1024 * 1024, transcendentals=0),
        name="pack",
    )(place, *pieces, weights)


def z_ring(value, shift):
    return lax.ppermute(value, "z", [(i, (i + shift) % 8) for i in range(8)])


def gather_bricks(low, high):
    pieces = {(0, 0): low, (0, 1): high}
    for step in range(1, 4):
        for half in range(2):
            for way in (-1, 1):
                pieces[way * step, half] = z_ring(pieces[way * (step - 1), half], -way)
    pieces[4, 0] = z_ring(pieces[-3, 0], 1)
    pieces[4, 1] = z_ring(pieces[3, 1], -1)
    mine = [pieces[shift, half] for shift in SHIFTS for half in range(2)]
    return mine + [lax.ppermute(piece, "c", [(0, 1), (1, 0)]) for piece in mine]


def per_device(field, brick_speed, send_index, send_count, weights, propagator):
    first = lax.axis_index("yl") == 0
    chosen = send_index[0]
    slots = lax.broadcasted_iota(jnp.int32, chosen.shape, 1)
    chosen = jnp.where(slots < send_count[0][:, None], chosen, -1).astype(jnp.bfloat16)
    chosen = chosen.reshape(8, 8, 2, CAP).transpose(0, 2, 1, 3).reshape(16, BCOL)
    chosen = jnp.pad(chosen, ((0, 0), (0, DEPTH - BCOL)))
    low = jnp.concatenate([brick_speed[: BCOL // 2], chosen])
    pieces = gather_bricks(low, brick_speed[BCOL // 2 :])

    moved = weights.reshape(2 * ROWS, STEPS, 8, 8, 64).transpose(3, 1, 0, 2, 4).reshape(PLANE, STEPS * 2 * ROWS, SLOTS)
    moved = lax.all_to_all(moved, ("x", "yh"), split_axis=0, concat_axis=0, tiled=True)

    place = jnp.stack([lax.axis_index("z"), lax.axis_index("c")]).astype(jnp.int32)
    partial = pack(place, pieces, moved).reshape(2 * PLANE, STEPS * ROWS, DEPTH)
    partial = lax.all_to_all(partial, ("x", "yh", "yl"), split_axis=0, concat_axis=0, tiled=True)
    code = partial.reshape(PLANE, 2, STEPS * ROWS, DEPTH).astype(jnp.int32).sum(0)
    code = jnp.concatenate([code[0], code[1]], 1)
    code = (((code + 32768) & 65535) - 32768).astype(jnp.int16).reshape(STEPS, ROWS, NZ)

    own = own_rows_all_depths(first, field.transpose(1, 0, 2), 1, 2)
    own_left, own_right = with_halo(own)
    code_left, code_right = with_halo(code)

    side = jnp.where(first, 0, 1).astype(jnp.int32).reshape(1)
    keep, send = march(
        side,
        code.reshape(STEPS * ROWS, NZ),
        code_left.reshape(STEPS * HALO, NZ),
        code_right.reshape(STEPS * HALO, NZ),
        own,
        own_left,
        own_right,
        propagator,
    )
    other = swap_dep(send).astype(jnp.float32)
    out = jnp.where(first, jnp.concatenate([keep, other], 1), jnp.concatenate([other, keep], 1))
    return out.transpose(1, 0, 2)


def solution(mesh):
    inner = Mesh(mesh.devices.reshape(SIZES), AXES)
    placed = (
        P(SECTOR, None, "yl"),
        P(SECTOR, "yl"),
        P(SECTOR, None, None),
        P(SECTOR, None),
        P(SECTOR, None, None),
        P(),
    )
    return jax.shard_map(
        per_device, mesh=inner, in_specs=placed, out_specs=P(SECTOR, None, "yl"), check_vma=False
    )
```

```python
import math

import jax
import jax.numpy as jnp
from jax import lax
from jax.experimental import pallas as pl
from jax.experimental.pallas import tpu as pltpu
from jax.sharding import Mesh, PartitionSpec as P

angle_rate = 200.0 / 1500.0
couple_real = 0.1
couple_imag = 0.15

AXES = ("z", "x", "yh", "c", "yl")
SECTOR = ("z", "x", "yh", "c")
SIZES = (8, 4, 2, 2, 2)
HALO = 8
ROWS = 32
EXT = ROWS + 2 * HALO
NZ = 1024
STEPS = 4
FACTORS = 2
RING = 256
VMEM = pl.BlockSpec(memory_space=pltpu.VMEM)
SMEM = pl.BlockSpec(memory_space=pltpu.SMEM)


def turn_code(speed):
    turns = speed * (-angle_rate / (2.0 * math.pi))
    code = jnp.round((turns - jnp.round(turns)) * 65536.0).astype(jnp.int32)
    return jnp.where(code > 32767, -32768, code)


def cos_sin(code):
    quadrant = (code + 8192) >> 14
    part = (code - (quadrant << 14)).astype(jnp.float32) * (1.0 / 16384.0)
    square = part * part
    h = math.pi / 2
    sine = part * (h + square * (-(h**3) / 6 + square * (h**5 / 120 - square * (h**7 / 5040))))
    cosine = 1.0 + square * (
        -(h**2) / 2 + square * (h**4 / 24 + square * (-(h**6) / 720 + square * (h**8 / 40320)))
    )
    odd = (quadrant & 1) == 1
    first = jnp.where(odd, sine, cosine)
    second = jnp.where(odd, cosine, sine)
    first = jnp.where(((quadrant + 1) & 2) == 2, -first, first)
    second = jnp.where((quadrant & 2) == 2, -second, second)
    return first, second


def march_kernel(
    side, code, code_left, code_right, field, field_left, field_right, factors_hbm, keep, send, *scratch
):
    state, padded, rounded, codes, factors, arrived = scratch
    copies = [pltpu.make_async_copy(factors_hbm.at[i], factors.at[i], arrived.at[i]) for i in range(FACTORS)]
    for copy in copies:
        copy.start()
    state[:, 0:HALO] = field_left[...]
    state[:, HALO : HALO + ROWS] = field[...]
    state[:, HALO + ROWS : EXT] = field_right[...]
    padded[:, 0:HALO] = jnp.zeros((2, HALO, NZ), jnp.float32)
    padded[:, HALO + EXT :] = jnp.zeros((2, HALO, NZ), jnp.float32)
    edge, body = STEPS * HALO, STEPS * ROWS
    for chunk in range(NZ // 128):
        lanes = slice(chunk * 128, (chunk + 1) * 128)
        codes[chunk, 0:edge] = code_left[:, lanes].astype(jnp.int32)
        codes[chunk, edge : edge + body] = ((code[:, lanes] + 32768) & 65535) - 32768
        codes[chunk, edge + body :] = code_right[:, lanes].astype(jnp.int32)
    for step in range(STEPS):
        for chunk in range(NZ // 128):
            lanes = slice(chunk * 128, (chunk + 1) * 128)
            cosine, sine = cos_sin(codes[chunk, pl.ds(step, EXT, stride=STEPS), :])
            real = state[0, :, lanes]
            imag = state[1, :, lanes]
            padded[0, HALO : HALO + EXT, lanes] = real * cosine - imag * sine
            padded[1, HALO : HALO + EXT, lanes] = real * sine + imag * cosine
        laplace = []
        for part in range(2):
            near = padded[part, HALO - 1 : HALO - 1 + EXT] + padded[part, HALO + 1 : HALO + 1 + EXT]
            far = padded[part, HALO - 2 : HALO - 2 + EXT] + padded[part, HALO + 2 : HALO + 2 + EXT]
            centre = padded[part, HALO : HALO + EXT]
            laplace.append((16.0 * near - far - 30.0 * centre) * (1.0 / 12.0))
        rounded[0:EXT] = (
            padded[0, HALO : HALO + EXT] + couple_real * laplace[0] - couple_imag * laplace[1]
        ).astype(jnp.bfloat16)
        rounded[EXT : 2 * EXT] = (
            padded[1, HALO : HALO + EXT] + couple_real * laplace[1] + couple_imag * laplace[0]
        ).astype(jnp.bfloat16)
        for factor in range(FACTORS):
            if step == 0:
                copies[factor].wait()
            left = rounded[...]
            for column in range(0, NZ, 256):
                by_real = jnp.dot(
                    left, factors[factor, 0, :, column : column + 256], preferred_element_type=jnp.float32
                )
                by_imag = jnp.dot(
                    left, factors[factor, 1, :, column : column + 256], preferred_element_type=jnp.float32
                )
                state[0, :, column : column + 256] = by_real[:EXT] - by_imag[EXT:]
                state[1, :, column : column + 256] = by_imag[:EXT] + by_real[EXT:]
            if factor + 1 < FACTORS:
                rounded[0:EXT] = state[0].astype(jnp.bfloat16)
                rounded[EXT : 2 * EXT] = state[1].astype(jnp.bfloat16)
    low = state[:, HALO : HALO + ROWS, 0 : NZ // 2]
    high = state[:, HALO : HALO + ROWS, NZ // 2 :]
    first = side[0] == 0
    keep[...] = jnp.where(first, low, high)
    send[...] = jnp.where(first, high, low).astype(jnp.bfloat16)


def march(side, code, code_left, code_right, field, field_left, field_right, factors):
    half = (2, ROWS, NZ // 2)
    return pl.pallas_call(
        march_kernel,
        out_shape=(jax.ShapeDtypeStruct(half, jnp.float32), jax.ShapeDtypeStruct(half, jnp.bfloat16)),
        in_specs=[SMEM] + [VMEM] * 6 + [pl.BlockSpec(memory_space=pl.ANY)],
        out_specs=(VMEM, VMEM),
        scratch_shapes=[
            pltpu.VMEM((2, EXT, NZ), jnp.float32),
            pltpu.VMEM((2, EXT + 2 * HALO, NZ), jnp.float32),
            pltpu.VMEM((2 * EXT, NZ), jnp.bfloat16),
            pltpu.VMEM((NZ // 128, STEPS * EXT, 128), jnp.int32),
            pltpu.VMEM((FACTORS, 2, NZ, NZ), jnp.bfloat16),
            pltpu.SemaphoreType.DMA((FACTORS,)),
        ],
        compiler_params=pltpu.CompilerParams(vmem_limit_bytes=40 * 1024 * 1024),
        cost_estimate=pl.CostEstimate(
            flops=2 * 8 * 2 * EXT * NZ * 2 * NZ, bytes_accessed=10 * 1024 * 1024, transcendentals=0
        ),
        name="march",
    )(side, code, code_left, code_right, field, field_left, field_right, factors)


def swap_dep(value):
    return lax.ppermute(value, "yl", [(0, 1), (1, 0)])


def ring_step(value, shift):
    return lax.ppermute(value, AXES, [(i, (i + shift) % RING) for i in range(RING)])


def own_rows_all_depths(first, value, dim, depth_dim):
    top = lax.slice_in_dim(value, 0, ROWS, axis=dim)
    bottom = lax.slice_in_dim(value, ROWS, 2 * ROWS, axis=dim)
    mine = jnp.where(first, top, bottom)
    other = swap_dep(jnp.where(first, bottom, top))
    return jnp.where(
        first, jnp.concatenate([mine, other], depth_dim), jnp.concatenate([other, mine], depth_dim)
    )


def with_halo(value, width):
    before = ring_step(value[:, -width:], 1)
    after = ring_step(value[:, :width], -1)
    return before, after


PLANE = 8
SLOTS = 512
BCOL = 256
CAP = 32
DEPTH = NZ // 2
EARLY = (0, -1, 1, -2, 2)
LATE = (-3, 3, 4)


def sort_kernel(weights, out):
    rows = weights.shape[0] * STEPS
    lane = lax.broadcasted_iota(jnp.int32, (rows, 128), 1)
    for pair in range(4):
        for x in range(4):
            both = []
            for z in (2 * pair, 2 * pair + 1):
                start = z * SLOTS + x * 128
                both.append(weights[:, :, start : start + 128].astype(jnp.float32).reshape(rows, 128))
            even, odd = both
            out[2 * x, :, pair * 128 : pair * 128 + 128] = jnp.where(
                lane < 64, even, pltpu.roll(odd, 64, 1)
            ).astype(jnp.bfloat16)
            out[2 * x + 1, :, pair * 128 : pair * 128 + 128] = jnp.where(
                lane < 64, pltpu.roll(even, 64, 1), odd
            ).astype(jnp.bfloat16)


def sort_weights(weights):
    block = 16
    return pl.pallas_call(
        sort_kernel,
        out_shape=jax.ShapeDtypeStruct((PLANE, 2 * ROWS * STEPS, SLOTS), jnp.bfloat16),
        grid=(2 * ROWS // block,),
        in_specs=[pl.BlockSpec((block, STEPS, 8 * SLOTS), lambda i: (i, 0, 0))],
        out_specs=pl.BlockSpec((PLANE, block * STEPS, SLOTS), lambda i: (0, i, 0)),
        compiler_params=pltpu.CompilerParams(vmem_limit_bytes=12 * 1024 * 1024),
        cost_estimate=pl.CostEstimate(flops=0, bytes_accessed=4 * 1024 * 1024, transcendentals=0),
        name="sort",
    )(weights)


def pack_kernel(place, *refs):
    pieces, (mine, other) = refs[:-2], refs[-2:]
    z, core = place[0], place[1]
    line = lax.broadcasted_iota(jnp.int32, (16, BCOL), 0)
    column = lax.broadcasted_iota(jnp.int32, (BCOL // 2, 2 * BCOL), 0)
    for brick in range(len(pieces) // 2):
        low, high = pieces[2 * brick], pieces[2 * brick + 1]
        table = low[BCOL // 2 :, 0:BCOL].astype(jnp.float32)
        index = jnp.concatenate(
            [
                jnp.sum(jnp.where(line == z * 2 + target, table, 0.0), axis=0, keepdims=True)
                for target in (core, 1 - core)
            ],
            axis=1,
        ).astype(jnp.int32)
        total = None
        for half, ref in enumerate((low, high)):
            onehot = jnp.where(column + half * (BCOL // 2) == index, 1.0, 0.0).astype(jnp.bfloat16)
            part = lax.dot_general(
                onehot, ref[0 : BCOL // 2, :], (((0,), (0,)), ((), ())), preferred_element_type=jnp.float32
            )
            total = part if total is None else total + part
        total = total.astype(jnp.bfloat16)
        span = slice(brick * CAP, (brick + 1) * CAP)
        mine[:, span, :] = total[:BCOL].reshape(PLANE, CAP, DEPTH)
        other[:, span, :] = total[BCOL:].reshape(PLANE, CAP, DEPTH)


def pack(place, pieces):
    bricks = len(pieces) // 2
    shape = jax.ShapeDtypeStruct((PLANE, bricks * CAP, DEPTH), jnp.bfloat16)
    return pl.pallas_call(
        pack_kernel,
        out_shape=(shape, shape),
        in_specs=[SMEM] + [VMEM] * len(pieces),
        out_specs=(VMEM, VMEM),
        compiler_params=pltpu.CompilerParams(vmem_limit_bytes=12 * 1024 * 1024),
        cost_estimate=pl.CostEstimate(
            flops=bricks * 2 * 512 * 256 * 512, bytes_accessed=bricks * 768 * 1024, transcendentals=0
        ),
        name="pack",
    )(place, *pieces)


def partial_kernel(place, *refs):
    groups, (weights, out, packed) = refs[:4], refs[4:]
    z, core = place[0], place[1]
    for group, ref in enumerate(groups):
        from_core = core if group < 2 else 1 - core
        for brick, shift in enumerate(LATE if group % 2 else EARLY):
            from_z = lax.rem(z + shift + 8, 8)
            start = pl.multiple_of((from_z * 2 + from_core) * CAP, CAP)
            packed[:, pl.ds(start, CAP), :] = ref[:, brick * CAP : (brick + 1) * CAP, :]
    for sector in range(PLANE):
        code = turn_code(jnp.dot(weights[sector], packed[sector], preferred_element_type=jnp.float32))
        out[sector] = code.astype(jnp.int16).reshape(2, STEPS * ROWS, DEPTH)


def partial_codes(place, groups, weights):
    return pl.pallas_call(
        partial_kernel,
        out_shape=jax.ShapeDtypeStruct((PLANE, 2, STEPS * ROWS, DEPTH), jnp.int16),
        in_specs=[SMEM] + [VMEM] * 5,
        out_specs=VMEM,
        scratch_shapes=[pltpu.VMEM((PLANE, SLOTS, DEPTH), jnp.bfloat16)],
        compiler_params=pltpu.CompilerParams(vmem_limit_bytes=20 * 1024 * 1024),
        cost_estimate=pl.CostEstimate(flops=2 * 537_000_000, bytes_accessed=8 * 1024 * 1024, transcendentals=0),
        name="partial",
    )(place, *groups, weights)


def sum_kernel(parts, out):
    for half in range(2):
        total = parts[0, half].astype(jnp.int32)
        for source in range(1, PLANE):
            total = total + parts[source, half].astype(jnp.int32)
        out[:, half * DEPTH : (half + 1) * DEPTH] = total


def sum_codes(parts):
    return pl.pallas_call(
        sum_kernel,
        out_shape=jax.ShapeDtypeStruct((STEPS * ROWS, NZ), jnp.int32),
        in_specs=[VMEM],
        out_specs=VMEM,
        compiler_params=pltpu.CompilerParams(vmem_limit_bytes=12 * 1024 * 1024),
        cost_estimate=pl.CostEstimate(flops=2_000_000, bytes_accessed=2_500_000, transcendentals=0),
        name="sums",
    )(parts)


def edge_codes(parts):
    code = parts.astype(jnp.int32).sum(0)
    code = jnp.concatenate([code[0], code[1]], 1)
    return (((code + 32768) & 65535) - 32768).astype(jnp.int16)


def z_ring(value, shift):
    return lax.ppermute(value, "z", [(i, (i + shift) % 8) for i in range(8)])


def swap_core(value):
    return lax.ppermute(value, "c", [(0, 1), (1, 0)])


def gather_bricks(low, high):
    pieces = {(0, 0): low, (0, 1): high}
    for step in range(1, 4):
        for half in range(2):
            for way in (-1, 1):
                pieces[way * step, half] = z_ring(pieces[way * (step - 1), half], -way)
    pieces[4, 0] = z_ring(pieces[-3, 0], 1)
    pieces[4, 1] = z_ring(pieces[3, 1], -1)
    return pieces


def per_device(field, brick_speed, send_index, send_count, weights, propagator):
    first = lax.axis_index("yl") == 0
    moved = sort_weights(weights)
    moved = lax.all_to_all(moved, ("x", "yh"), split_axis=0, concat_axis=0, tiled=True)

    chosen = send_index[0]
    slots = lax.broadcasted_iota(jnp.int32, chosen.shape, 1)
    chosen = jnp.where(slots < send_count[0][:, None], chosen, -1).astype(jnp.bfloat16)
    chosen = chosen.reshape(8, 8, 2, CAP).transpose(0, 2, 1, 3).reshape(16, BCOL)
    chosen = jnp.pad(chosen, ((0, 0), (0, DEPTH - BCOL)))
    low = jnp.concatenate([brick_speed[: BCOL // 2], chosen])
    pieces = gather_bricks(low, brick_speed[BCOL // 2 :])
    place = jnp.stack([lax.axis_index("z"), lax.axis_index("c")]).astype(jnp.int32)

    own = own_rows_all_depths(first, field.transpose(1, 0, 2), 1, 2)
    own_left, own_right = with_halo(own, HALO)

    mine_early, other_early = pack(place, [pieces[shift, half] for shift in EARLY for half in range(2)])
    other_early = swap_core(other_early)
    late = [pieces[shift, half] for shift in LATE for half in range(2)]
    late, own, own_left, own_right = lax.optimization_barrier((late, own, own_left, own_right))
    mine_late, other_late = pack(place, late)
    other_late = swap_core(other_late)
    parts = partial_codes(place, (mine_early, mine_late, other_early, other_late), moved)
    parts = lax.all_to_all(
        parts.reshape(2 * PLANE, STEPS * ROWS, DEPTH), ("x", "yh", "yl"), split_axis=0, concat_axis=0, tiled=True
    ).reshape(PLANE, 2, STEPS * ROWS, DEPTH)
    edge = STEPS * HALO
    code_left = ring_step(edge_codes(parts[:, :, -edge:]), 1)
    code_right = ring_step(edge_codes(parts[:, :, :edge]), -1)
    code = sum_codes(parts)

    side = jnp.where(first, 0, 1).astype(jnp.int32).reshape(1)
    keep, send = march(side, code, code_left, code_right, own, own_left, own_right, propagator)
    other = swap_dep(send).astype(jnp.float32)
    out = jnp.where(first, jnp.concatenate([keep, other], 1), jnp.concatenate([other, keep], 1))
    return out.transpose(1, 0, 2)


def solution(mesh):
    inner = Mesh(mesh.devices.reshape(SIZES), AXES)
    placed = (
        P(SECTOR, None, "yl"),
        P(SECTOR, "yl"),
        P(SECTOR, None, None),
        P(SECTOR, None),
        P(SECTOR, None, None),
        P(),
    )
    return jax.shard_map(
        per_device, mesh=inner, in_specs=placed, out_specs=P(SECTOR, None, "yl"), check_vma=False
    )
```

```python
import math

import jax
import jax.numpy as jnp
from jax import lax
from jax.experimental import pallas as pl
from jax.experimental.pallas import tpu as pltpu
from jax.sharding import Mesh, PartitionSpec as P

angle_rate = 200.0 / 1500.0
couple_real = 0.1
couple_imag = 0.15

AXES = ("z", "x", "yh", "c", "yl")
SECTOR = ("z", "x", "yh", "c")
SIZES = (8, 4, 2, 2, 2)
HALO = 8
ROWS = 32
EXT = ROWS + 2 * HALO
SHARED = ROWS + HALO
NZ = 1024
DEPTH = NZ // 2
STEPS = 4
FACTORS = 2
RING = 256
MIB = 1024 * 1024
VMEM = pl.BlockSpec(memory_space=pltpu.VMEM)
SMEM = pl.BlockSpec(memory_space=pltpu.SMEM)
ANY = pl.BlockSpec(memory_space=pl.ANY)


def turn_code(speed):
    turns = speed * (-angle_rate / (2.0 * math.pi))
    code = jnp.round((turns - jnp.round(turns)) * 65536.0).astype(jnp.int32)
    return jnp.where(code > 32767, -32768, code)


def cos_sin(code):
    quadrant = (code + 8192) >> 14
    part = (code - (quadrant << 14)).astype(jnp.float32) * (1.0 / 16384.0)
    square = part * part
    h = math.pi / 2
    sine = part * (h + square * (-(h**3) / 6 + square * (h**5 / 120 - square * (h**7 / 5040))))
    cosine = 1.0 + square * (
        -(h**2) / 2 + square * (h**4 / 24 + square * (-(h**6) / 720 + square * (h**8 / 40320)))
    )
    odd = (quadrant & 1) == 1
    first = jnp.where(odd, sine, cosine)
    second = jnp.where(odd, cosine, sine)
    first = jnp.where(((quadrant + 1) & 2) == 2, -first, first)
    second = jnp.where((quadrant & 2) == 2, -second, second)
    return first, second


def march_kernel(side, code, code_left, code_right, field, partner, near, far, factors, keep, send, *scratch):
    state, padded, rounded, codes = scratch
    second = side[0]
    first = second == 0
    rows = pl.ds(pl.multiple_of(HALO * (1 - second), HALO), SHARED)
    outer = pl.ds(pl.multiple_of(SHARED * second, HALO), HALO)
    here = pl.ds(pl.multiple_of(DEPTH * second, DEPTH), DEPTH)
    there = pl.ds(pl.multiple_of(DEPTH * (1 - second), DEPTH), DEPTH)
    state[:, rows, here] = field[:, pl.ds(pl.multiple_of((2 * ROWS - SHARED) * second, HALO), SHARED)]
    state[:, rows, there] = partner[...]
    state[:, outer, here] = far[...]
    state[:, outer, there] = near[...]
    padded[:, 0:HALO] = jnp.zeros((2, HALO, NZ), jnp.float32)
    padded[:, HALO + EXT :] = jnp.zeros((2, HALO, NZ), jnp.float32)
    edge, body = STEPS * HALO, STEPS * ROWS
    for chunk in range(NZ // 128):
        lanes = slice(chunk * 128, (chunk + 1) * 128)
        codes[chunk, 0:edge] = code_left[:, lanes].astype(jnp.int32)
        codes[chunk, edge : edge + body] = ((code[:, lanes] + 32768) & 65535) - 32768
        codes[chunk, edge + body :] = code_right[:, lanes].astype(jnp.int32)
    for step in range(STEPS):
        for chunk in range(NZ // 128):
            lanes = slice(chunk * 128, (chunk + 1) * 128)
            cosine, sine = cos_sin(codes[chunk, pl.ds(step, EXT, stride=STEPS), :])
            real = state[0, :, lanes]
            imag = state[1, :, lanes]
            padded[0, HALO : HALO + EXT, lanes] = real * cosine - imag * sine
            padded[1, HALO : HALO + EXT, lanes] = real * sine + imag * cosine
        laplace = []
        for part in range(2):
            near = padded[part, HALO - 1 : HALO - 1 + EXT] + padded[part, HALO + 1 : HALO + 1 + EXT]
            far = padded[part, HALO - 2 : HALO - 2 + EXT] + padded[part, HALO + 2 : HALO + 2 + EXT]
            centre = padded[part, HALO : HALO + EXT]
            laplace.append((16.0 * near - far - 30.0 * centre) * (1.0 / 12.0))
        rounded[0:EXT] = (
            padded[0, HALO : HALO + EXT] + couple_real * laplace[0] - couple_imag * laplace[1]
        ).astype(jnp.bfloat16)
        rounded[EXT : 2 * EXT] = (
            padded[1, HALO : HALO + EXT] + couple_real * laplace[1] + couple_imag * laplace[0]
        ).astype(jnp.bfloat16)
        for factor in range(FACTORS):
            left = rounded[...]
            for column in range(0, NZ, 256):
                by_real = jnp.dot(
                    left, factors[factor, 0, :, column : column + 256], preferred_element_type=jnp.float32
                )
                by_imag = jnp.dot(
                    left, factors[factor, 1, :, column : column + 256], preferred_element_type=jnp.float32
                )
                state[0, :, column : column + 256] = by_real[:EXT] - by_imag[EXT:]
                state[1, :, column : column + 256] = by_imag[:EXT] + by_real[EXT:]
            if factor + 1 < FACTORS:
                rounded[0:EXT] = state[0].astype(jnp.bfloat16)
                rounded[EXT : 2 * EXT] = state[1].astype(jnp.bfloat16)
    low = state[:, HALO : HALO + ROWS, 0:DEPTH]
    high = state[:, HALO : HALO + ROWS, DEPTH:NZ]
    keep[...] = jnp.where(first, low, high)
    send[...] = jnp.where(first, high, low).astype(jnp.bfloat16)


def march(side, code, code_left, code_right, field, partner, near, far, factors):
    return pl.pallas_call(
        march_kernel,
        out_shape=(
            jax.ShapeDtypeStruct((2, ROWS, DEPTH), jnp.float32),
            jax.ShapeDtypeStruct((2, ROWS, DEPTH), jnp.bfloat16),
        ),
        in_specs=[SMEM] + [VMEM] * 8,
        out_specs=(VMEM, VMEM),
        scratch_shapes=[
            pltpu.VMEM((2, EXT, NZ), jnp.float32),
            pltpu.VMEM((2, EXT + 2 * HALO, NZ), jnp.float32),
            pltpu.VMEM((2 * EXT, NZ), jnp.bfloat16),
            pltpu.VMEM((NZ // 128, STEPS * EXT, 128), jnp.int32),
        ],
        compiler_params=pltpu.CompilerParams(vmem_limit_bytes=24 * MIB),
        cost_estimate=pl.CostEstimate(
            flops=2 * 8 * 2 * EXT * NZ * 2 * NZ, bytes_accessed=10 * 1024 * 1024, transcendentals=0
        ),
        name="march",
    )(side, code, code_left, code_right, field, partner, near, far, factors)


def merge_kernel(side, keep, other, out):
    for part in range(2):
        out[pl.ds(side[0] * ROWS, ROWS), part, :] = keep[part]
        out[pl.ds((1 - side[0]) * ROWS, ROWS), part, :] = other[part].astype(jnp.float32)


def merge(side, keep, other):
    return pl.pallas_call(
        merge_kernel,
        out_shape=jax.ShapeDtypeStruct((2 * ROWS, 2, DEPTH), jnp.float32),
        in_specs=[SMEM, VMEM, VMEM],
        out_specs=VMEM,
        compiler_params=pltpu.CompilerParams(vmem_limit_bytes=12 * MIB),
        name="merge",
    )(side, keep, other)


def swap_dep(value):
    return lax.ppermute(value, "yl", [(0, 1), (1, 0)])


def ring_step(value, shift):
    return lax.ppermute(value, AXES, [(i, (i + shift) % RING) for i in range(RING)])


def exchange_field(first, field):
    top, bottom = field[:, :HALO], field[:, -HALO:]
    partner = swap_dep(jnp.where(first, field[:, -SHARED:], field[:, :SHARED]))
    across = [(i, i + 1 if i % 2 else i - 1) for i in range(RING)]
    near = lax.ppermute(jnp.where(first, top, bottom), AXES, [(i, j % RING) for i, j in across])
    along = [(i, i - 2 if i % 2 else i + 2) for i in range(RING)]
    far = lax.ppermute(jnp.where(first, bottom, top), AXES, [(i, j % RING) for i, j in along])
    return partner, near, far


PLANE = 8
SLOTS = 512
BCOL = 256
CAP = 32
EARLY = (0, -1, 1, -2, 2)
LATE = (-3, 3, 4)


def sort_kernel(weights, out):
    rows = weights.shape[0] * STEPS
    lane = lax.broadcasted_iota(jnp.int32, (rows, 128), 1)
    for pair in range(4):
        for x in range(4):
            both = []
            for z in (2 * pair, 2 * pair + 1):
                start = z * SLOTS + x * 128
                both.append(weights[:, :, start : start + 128].astype(jnp.float32).reshape(rows, 128))
            even, odd = both
            out[2 * x, :, pair * 128 : pair * 128 + 128] = jnp.where(
                lane < 64, even, pltpu.roll(odd, 64, 1)
            ).astype(jnp.bfloat16)
            out[2 * x + 1, :, pair * 128 : pair * 128 + 128] = jnp.where(
                lane < 64, pltpu.roll(even, 64, 1), odd
            ).astype(jnp.bfloat16)


def sort_weights(weights):
    block = 16
    return pl.pallas_call(
        sort_kernel,
        out_shape=jax.ShapeDtypeStruct((PLANE, 2 * ROWS * STEPS, SLOTS), jnp.bfloat16),
        grid=(2 * ROWS // block,),
        in_specs=[pl.BlockSpec((block, STEPS, 8 * SLOTS), lambda i: (i, 0, 0))],
        out_specs=pl.BlockSpec((PLANE, block * STEPS, SLOTS), lambda i: (0, i, 0)),
        compiler_params=pltpu.CompilerParams(vmem_limit_bytes=12 * MIB),
        cost_estimate=pl.CostEstimate(flops=0, bytes_accessed=4 * 1024 * 1024, transcendentals=0),
        name="sort",
    )(weights)


def pack_kernel(place, *refs):
    pieces, (mine, other, held, rows, came, left) = refs[:-6], refs[-6:]
    bricks = held.shape[0]
    per_brick = len(pieces) // bricks
    arrivals = []
    for i in range(bricks):
        start, pair = 0, []
        for j, piece in enumerate(pieces[per_brick * i : per_brick * (i + 1)]):
            target = held.at[i, start : start + piece.shape[0]]
            pair.append(pltpu.make_async_copy(piece, target, came.at[i, j]))
            start += piece.shape[0]
        arrivals.append(pair)
    for pair in arrivals:
        for copy in pair:
            copy.start()
    z, core = place[0], place[1]
    line = lax.broadcasted_iota(jnp.int32, (16, BCOL), 0)
    column = lax.broadcasted_iota(jnp.int32, (BCOL // 2, 2 * BCOL), 0)
    departures = []
    for brick in range(bricks):
        for copy in arrivals[brick]:
            copy.wait()
        table = held[brick, 0:16, 0:BCOL].astype(jnp.float32)
        index = jnp.concatenate(
            [
                jnp.sum(jnp.where(line == z * 2 + target, table, 0.0), axis=0, keepdims=True)
                for target in (core, 1 - core)
            ],
            axis=1,
        ).astype(jnp.int32)
        total = None
        for half in range(2):
            onehot = jnp.where(column + half * (BCOL // 2) == index, 1.0, 0.0).astype(jnp.bfloat16)
            start = 16 + half * (BCOL // 2)
            part = lax.dot_general(
                onehot,
                held[brick, start : start + BCOL // 2, :],
                (((0,), (0,)), ((), ())),
                preferred_element_type=jnp.float32,
            )
            total = part if total is None else total + part
        total = total.astype(jnp.bfloat16)
        span = slice(brick * CAP, (brick + 1) * CAP)
        for target, out in enumerate((mine, other)):
            rows[target, :, span, :] = total[target * BCOL : (target + 1) * BCOL].reshape(PLANE, CAP, DEPTH)
            copy = pltpu.make_async_copy(rows.at[target, :, span, :], out.at[:, span, :], left.at[brick, target])
            copy.start()
            departures.append(copy)
    for copy in departures:
        copy.wait()


def pack(place, pieces, bricks, room):
    shape = jax.ShapeDtypeStruct((PLANE, bricks * CAP, DEPTH), jnp.bfloat16)
    return pl.pallas_call(
        pack_kernel,
        out_shape=(shape, shape),
        in_specs=[SMEM] + [ANY] * len(pieces),
        out_specs=(ANY, ANY),
        scratch_shapes=[
            pltpu.VMEM((bricks, BCOL + 16, DEPTH), jnp.bfloat16),
            pltpu.VMEM((2, PLANE, bricks * CAP, DEPTH), jnp.bfloat16),
            pltpu.SemaphoreType.DMA((bricks, 2)),
            pltpu.SemaphoreType.DMA((bricks, 2)),
        ],
        compiler_params=pltpu.CompilerParams(vmem_limit_bytes=room),
        cost_estimate=pl.CostEstimate(flops=bricks * 400_000_000, bytes_accessed=1024, transcendentals=0),
        name="pack",
    )(place, *pieces)


def partial_kernel(place, *refs):
    groups, (weights, out, packed) = refs[:4], refs[4:]
    z, core = place[0], place[1]
    for group, ref in enumerate(groups):
        from_core = core if group < 2 else 1 - core
        for brick, shift in enumerate(LATE if group % 2 else EARLY):
            from_z = lax.rem(z + shift + 8, 8)
            start = pl.multiple_of((from_z * 2 + from_core) * CAP, CAP)
            packed[:, pl.ds(start, CAP), :] = ref[:, brick * CAP : (brick + 1) * CAP, :]
    for sector in range(PLANE):
        code = turn_code(jnp.dot(weights[sector], packed[sector], preferred_element_type=jnp.float32))
        out[sector] = code.astype(jnp.int16).reshape(2, STEPS * ROWS, DEPTH)


def partial_codes(place, groups, weights):
    return pl.pallas_call(
        partial_kernel,
        out_shape=jax.ShapeDtypeStruct((PLANE, 2, STEPS * ROWS, DEPTH), jnp.int16),
        in_specs=[SMEM] + [VMEM] * 5,
        out_specs=VMEM,
        scratch_shapes=[pltpu.VMEM((PLANE, SLOTS, DEPTH), jnp.bfloat16)],
        compiler_params=pltpu.CompilerParams(vmem_limit_bytes=20 * MIB),
        cost_estimate=pl.CostEstimate(flops=2 * 537_000_000, bytes_accessed=8 * 1024 * 1024, transcendentals=0),
        name="partial",
    )(place, *groups, weights)


def sum_kernel(parts, out):
    for half in range(2):
        total = parts[0, half].astype(jnp.int32)
        for source in range(1, PLANE):
            total = total + parts[source, half].astype(jnp.int32)
        out[:, half * DEPTH : (half + 1) * DEPTH] = total


def sum_codes(parts):
    return pl.pallas_call(
        sum_kernel,
        out_shape=jax.ShapeDtypeStruct((STEPS * ROWS, NZ), jnp.int32),
        in_specs=[VMEM],
        out_specs=VMEM,
        compiler_params=pltpu.CompilerParams(vmem_limit_bytes=12 * MIB),
        cost_estimate=pl.CostEstimate(flops=2_000_000, bytes_accessed=2_500_000, transcendentals=0),
        name="sums",
    )(parts)


def edge_codes(parts):
    code = parts.astype(jnp.int32).sum(0)
    code = jnp.concatenate([code[0], code[1]], 1)
    return (((code + 32768) & 65535) - 32768).astype(jnp.int16)


def z_ring(value, shift):
    return lax.ppermute(value, "z", [(i, (i + shift) % 8) for i in range(8)])


def swap_core(value):
    return lax.ppermute(value, "c", [(0, 1), (1, 0)])


def first_step(brick):
    return z_ring(brick, 1), z_ring(brick, -1)


def gather_and_pack(place, brick, before, after):
    whole = {0: brick, -1: before, 1: after}
    for step in range(2, 4):
        for way in (-1, 1):
            whole[way * step] = z_ring(whole[way * (step - 1)], -way)
    early = pack(place, [whole[shift] for shift in EARLY], len(EARLY), 56 * MIB)
    early, whole[-3], whole[3] = lax.optimization_barrier((early, whole[-3], whole[3]))
    mine_early, other_early = early
    whole[4] = z_ring(whole[-3], 1)
    other_early = swap_core(other_early)
    mine_late, other_late = pack(place, [whole[shift] for shift in LATE], len(LATE), 12 * MIB)
    other_late = swap_core(other_late)
    return mine_early, mine_late, other_early, other_late


def nothing_packed(place, brick, before, after):
    rows = [jnp.zeros((PLANE, len(group) * CAP, DEPTH), brick.dtype) for group in (EARLY, LATE)]
    return rows[0], rows[1], rows[0], rows[1]


def per_device(field, brick_speed, send_index, send_count, weights, propagator):
    slots = lax.broadcasted_iota(jnp.int32, send_index.shape, 2)
    chosen = jnp.where(slots < send_count[:, :, None], send_index, -1).astype(jnp.bfloat16)
    chosen = chosen.reshape(8, 8, 2, CAP).transpose(0, 2, 1, 3).reshape(16, BCOL)
    brick = jnp.concatenate([jnp.pad(chosen, ((0, 0), (0, DEPTH - BCOL))), brick_speed])
    place = jnp.stack([lax.axis_index("z"), lax.axis_index("c")]).astype(jnp.int32)
    side = lax.axis_index("yl").astype(jnp.int32).reshape(1)
    brick, place, side = lax.optimization_barrier((brick, place, side))
    first = side[0] == 0

    before, after = first_step(brick)
    before, after, moved = lax.optimization_barrier((before, after, sort_weights(weights)))
    moved = lax.all_to_all(moved, ("x", "yh"), split_axis=0, concat_axis=0, tiled=True)
    groups = lax.cond(
        send_count[0, 0] <= CAP, gather_and_pack, nothing_packed, place, brick, before, after
    )
    parts = partial_codes(place, groups, moved)

    field, parts = lax.optimization_barrier((field.transpose(1, 0, 2), parts))
    partner, near, far = exchange_field(first, field)
    parts = lax.all_to_all(
        parts.reshape(2 * PLANE, STEPS * ROWS, DEPTH), ("x", "yh", "yl"), split_axis=0, concat_axis=0, tiled=True
    ).reshape(PLANE, 2, STEPS * ROWS, DEPTH)
    parts, partner, near, far = lax.optimization_barrier((parts, partner, near, far))
    edge = STEPS * HALO
    edges = (edge_codes(parts[:, :, -edge:]), edge_codes(parts[:, :, :edge]))
    code_left, code_right = ring_step(edges[0], 1), ring_step(edges[1], -1)
    code = sum_codes(parts)

    keep, send = march(side, code, code_left, code_right, field, partner, near, far, propagator)
    return merge(side, keep, swap_dep(send))


def solution(mesh):
    inner = Mesh(mesh.devices.reshape(SIZES), AXES)
    placed = (
        P(SECTOR, None, "yl"),
        P(SECTOR, "yl"),
        P(SECTOR, None, None),
        P(SECTOR, None),
        P(SECTOR, None, None),
        P(),
    )
    return jax.shard_map(
        per_device, mesh=inner, in_specs=placed, out_specs=P(SECTOR, None, "yl"), check_vma=False
    )
```

```python
import math

import jax
import jax.numpy as jnp
from jax import lax
from jax.experimental import pallas as pl
from jax.experimental.pallas import tpu as pltpu
from jax.sharding import Mesh, PartitionSpec as P

angle_rate = 200.0 / 1500.0
couple_real = 0.1
couple_imag = 0.15

AXES = ("z", "x", "yh", "c", "yl")
SECTOR = ("z", "x", "yh", "c")
SIZES = (8, 4, 2, 2, 2)
HALO = 8
ROWS = 32
EXT = ROWS + 2 * HALO
SHARED = ROWS + HALO
NZ = 1024
DEPTH = NZ // 2
STEPS = 4
FACTORS = 2
RING = 256
MIB = 1024 * 1024
VMEM = pl.BlockSpec(memory_space=pltpu.VMEM)
SMEM = pl.BlockSpec(memory_space=pltpu.SMEM)
ANY = pl.BlockSpec(memory_space=pl.ANY)


def turn_code(speed):
    turns = speed * (-angle_rate / (2.0 * math.pi))
    code = jnp.round((turns - jnp.round(turns)) * 65536.0).astype(jnp.int32)
    return jnp.where(code > 32767, -32768, code)


def cos_sin(code):
    quadrant = (code + 8192) >> 14
    part = (code - (quadrant << 14)).astype(jnp.float32) * (1.0 / 16384.0)
    square = part * part
    h = math.pi / 2
    sine = part * (h + square * (-(h**3) / 6 + square * (h**5 / 120 - square * (h**7 / 5040))))
    cosine = 1.0 + square * (
        -(h**2) / 2 + square * (h**4 / 24 + square * (-(h**6) / 720 + square * (h**8 / 40320)))
    )
    odd = (quadrant & 1) == 1
    first = jnp.where(odd, sine, cosine)
    second = jnp.where(odd, cosine, sine)
    first = jnp.where(((quadrant + 1) & 2) == 2, -first, first)
    second = jnp.where((quadrant & 2) == 2, -second, second)
    return first, second


def march_kernel(side, code, code_left, code_right, field, partner, near, far, factors, keep, send, *scratch):
    state, padded, rounded, codes = scratch
    second = side[0]
    first = second == 0
    rows = pl.ds(pl.multiple_of(HALO * (1 - second), HALO), SHARED)
    outer = pl.ds(pl.multiple_of(SHARED * second, HALO), HALO)
    here = pl.ds(pl.multiple_of(DEPTH * second, DEPTH), DEPTH)
    there = pl.ds(pl.multiple_of(DEPTH * (1 - second), DEPTH), DEPTH)
    state[:, rows, here] = field[:, pl.ds(pl.multiple_of((2 * ROWS - SHARED) * second, HALO), SHARED)]
    state[:, rows, there] = partner[...]
    state[:, outer, here] = far[...]
    state[:, outer, there] = near[...]
    padded[:, 0:HALO] = jnp.zeros((2, HALO, NZ), jnp.float32)
    padded[:, HALO + EXT :] = jnp.zeros((2, HALO, NZ), jnp.float32)
    edge, body = STEPS * HALO, STEPS * ROWS
    for chunk in range(NZ // 128):
        lanes = slice(chunk * 128, (chunk + 1) * 128)
        codes[chunk, 0:edge] = code_left[:, lanes].astype(jnp.int32)
        codes[chunk, edge : edge + body] = ((code[:, lanes] + 32768) & 65535) - 32768
        codes[chunk, edge + body :] = code_right[:, lanes].astype(jnp.int32)
    for step in range(STEPS):
        for chunk in range(NZ // 128):
            lanes = slice(chunk * 128, (chunk + 1) * 128)
            cosine, sine = cos_sin(codes[chunk, pl.ds(step, EXT, stride=STEPS), :])
            real = state[0, :, lanes]
            imag = state[1, :, lanes]
            padded[0, HALO : HALO + EXT, lanes] = real * cosine - imag * sine
            padded[1, HALO : HALO + EXT, lanes] = real * sine + imag * cosine
        laplace = []
        for part in range(2):
            near = padded[part, HALO - 1 : HALO - 1 + EXT] + padded[part, HALO + 1 : HALO + 1 + EXT]
            far = padded[part, HALO - 2 : HALO - 2 + EXT] + padded[part, HALO + 2 : HALO + 2 + EXT]
            centre = padded[part, HALO : HALO + EXT]
            laplace.append((16.0 * near - far - 30.0 * centre) * (1.0 / 12.0))
        rounded[0:EXT] = (
            padded[0, HALO : HALO + EXT] + couple_real * laplace[0] - couple_imag * laplace[1]
        ).astype(jnp.bfloat16)
        rounded[EXT : 2 * EXT] = (
            padded[1, HALO : HALO + EXT] + couple_real * laplace[1] + couple_imag * laplace[0]
        ).astype(jnp.bfloat16)
        for factor in range(FACTORS):
            left = rounded[...]
            for column in range(0, NZ, 256):
                by_real = jnp.dot(
                    left, factors[factor, 0, :, column : column + 256], preferred_element_type=jnp.float32
                )
                by_imag = jnp.dot(
                    left, factors[factor, 1, :, column : column + 256], preferred_element_type=jnp.float32
                )
                state[0, :, column : column + 256] = by_real[:EXT] - by_imag[EXT:]
                state[1, :, column : column + 256] = by_imag[:EXT] + by_real[EXT:]
            if factor + 1 < FACTORS:
                rounded[0:EXT] = state[0].astype(jnp.bfloat16)
                rounded[EXT : 2 * EXT] = state[1].astype(jnp.bfloat16)
    low = state[:, HALO : HALO + ROWS, 0:DEPTH]
    high = state[:, HALO : HALO + ROWS, DEPTH:NZ]
    keep[...] = jnp.where(first, low, high)
    send[...] = jnp.where(first, high, low).astype(jnp.bfloat16)


def march(side, code, code_left, code_right, field, partner, near, far, factors):
    return pl.pallas_call(
        march_kernel,
        out_shape=(
            jax.ShapeDtypeStruct((2, ROWS, DEPTH), jnp.float32),
            jax.ShapeDtypeStruct((2, ROWS, DEPTH), jnp.bfloat16),
        ),
        in_specs=[SMEM] + [VMEM] * 8,
        out_specs=(VMEM, VMEM),
        scratch_shapes=[
            pltpu.VMEM((2, EXT, NZ), jnp.float32),
            pltpu.VMEM((2, EXT + 2 * HALO, NZ), jnp.float32),
            pltpu.VMEM((2 * EXT, NZ), jnp.bfloat16),
            pltpu.VMEM((NZ // 128, STEPS * EXT, 128), jnp.int32),
        ],
        compiler_params=pltpu.CompilerParams(vmem_limit_bytes=24 * MIB),
        cost_estimate=pl.CostEstimate(
            flops=2 * 8 * 2 * EXT * NZ * 2 * NZ, bytes_accessed=10 * 1024 * 1024, transcendentals=0
        ),
        name="march",
    )(side, code, code_left, code_right, field, partner, near, far, factors)


def merge_kernel(side, keep, other, out):
    for part in range(2):
        out[pl.ds(side[0] * ROWS, ROWS), part, :] = keep[part]
        out[pl.ds((1 - side[0]) * ROWS, ROWS), part, :] = other[part].astype(jnp.float32)


def merge(side, keep, other):
    return pl.pallas_call(
        merge_kernel,
        out_shape=jax.ShapeDtypeStruct((2 * ROWS, 2, DEPTH), jnp.float32),
        in_specs=[SMEM, VMEM, VMEM],
        out_specs=VMEM,
        compiler_params=pltpu.CompilerParams(vmem_limit_bytes=12 * MIB),
        name="merge",
    )(side, keep, other)


def swap_dep(value):
    return lax.ppermute(value, "yl", [(0, 1), (1, 0)])


def ring_step(value, shift):
    return lax.ppermute(value, AXES, [(i, (i + shift) % RING) for i in range(RING)])


def exchange_field(first, field):
    top, bottom = field[:, :HALO], field[:, -HALO:]
    partner = swap_dep(jnp.where(first, field[:, -SHARED:], field[:, :SHARED]))
    across = [(i, i + 1 if i % 2 else i - 1) for i in range(RING)]
    near = lax.ppermute(jnp.where(first, top, bottom), AXES, [(i, j % RING) for i, j in across])
    along = [(i, i - 2 if i % 2 else i + 2) for i in range(RING)]
    far = lax.ppermute(jnp.where(first, bottom, top), AXES, [(i, j % RING) for i, j in along])
    return partner, near, far


PLANE = 8
SLOTS = 512
BCOL = 256
CAP = 32
EARLY = (0, -1, 1, -2, 2)
LATE = (-3, 3, 4)


def sort_kernel(weights, out):
    rows = weights.shape[0] * STEPS
    lane = lax.broadcasted_iota(jnp.int32, (rows, 128), 1)
    for pair in range(4):
        for x in range(4):
            both = []
            for z in (2 * pair, 2 * pair + 1):
                start = z * SLOTS + x * 128
                both.append(weights[:, :, start : start + 128].astype(jnp.float32).reshape(rows, 128))
            even, odd = both
            out[2 * x, :, pair * 128 : pair * 128 + 128] = jnp.where(
                lane < 64, even, pltpu.roll(odd, 64, 1)
            ).astype(jnp.bfloat16)
            out[2 * x + 1, :, pair * 128 : pair * 128 + 128] = jnp.where(
                lane < 64, pltpu.roll(even, 64, 1), odd
            ).astype(jnp.bfloat16)


def sort_weights(weights):
    block = 16
    return pl.pallas_call(
        sort_kernel,
        out_shape=jax.ShapeDtypeStruct((PLANE, 2 * ROWS * STEPS, SLOTS), jnp.bfloat16),
        grid=(2 * ROWS // block,),
        in_specs=[pl.BlockSpec((block, STEPS, 8 * SLOTS), lambda i: (i, 0, 0))],
        out_specs=pl.BlockSpec((PLANE, block * STEPS, SLOTS), lambda i: (0, i, 0)),
        compiler_params=pltpu.CompilerParams(vmem_limit_bytes=12 * MIB),
        cost_estimate=pl.CostEstimate(flops=0, bytes_accessed=4 * 1024 * 1024, transcendentals=0),
        name="sort",
    )(weights)


def pack_kernel(place, *refs):
    pieces, (mine, other, held, rows, came, left) = refs[:-6], refs[-6:]
    bricks = held.shape[0]
    per_brick = len(pieces) // bricks
    arrivals = []
    for i in range(bricks):
        start, pair = 0, []
        for j, piece in enumerate(pieces[per_brick * i : per_brick * (i + 1)]):
            target = held.at[i, start : start + piece.shape[0]]
            pair.append(pltpu.make_async_copy(piece, target, came.at[i, j]))
            start += piece.shape[0]
        arrivals.append(pair)
    for pair in arrivals:
        for copy in pair:
            copy.start()
    z, core = place[0], place[1]
    line = lax.broadcasted_iota(jnp.int32, (16, BCOL), 0)
    column = lax.broadcasted_iota(jnp.int32, (BCOL // 2, 2 * BCOL), 0)
    departures = []
    for brick in range(bricks):
        for copy in arrivals[brick]:
            copy.wait()
        table = held[brick, 0:16, 0:BCOL].astype(jnp.float32)
        index = jnp.concatenate(
            [
                jnp.sum(jnp.where(line == z * 2 + target, table, 0.0), axis=0, keepdims=True)
                for target in (core, 1 - core)
            ],
            axis=1,
        ).astype(jnp.int32)
        total = None
        for half in range(2):
            onehot = jnp.where(column + half * (BCOL // 2) == index, 1.0, 0.0).astype(jnp.bfloat16)
            start = 16 + half * (BCOL // 2)
            part = lax.dot_general(
                onehot,
                held[brick, start : start + BCOL // 2, :],
                (((0,), (0,)), ((), ())),
                preferred_element_type=jnp.float32,
            )
            total = part if total is None else total + part
        total = total.astype(jnp.bfloat16)
        span = slice(brick * CAP, (brick + 1) * CAP)
        for target, out in enumerate((mine, other)):
            rows[target, :, span, :] = total[target * BCOL : (target + 1) * BCOL].reshape(PLANE, CAP, DEPTH)
            copy = pltpu.make_async_copy(rows.at[target, :, span, :], out.at[:, span, :], left.at[brick, target])
            copy.start()
            departures.append(copy)
    for copy in departures:
        copy.wait()


def pack(place, pieces, bricks, room):
    shape = jax.ShapeDtypeStruct((PLANE, bricks * CAP, DEPTH), jnp.bfloat16)
    return pl.pallas_call(
        pack_kernel,
        out_shape=(shape, shape),
        in_specs=[SMEM] + [ANY] * len(pieces),
        out_specs=(ANY, ANY),
        scratch_shapes=[
            pltpu.VMEM((bricks, BCOL + 16, DEPTH), jnp.bfloat16),
            pltpu.VMEM((2, PLANE, bricks * CAP, DEPTH), jnp.bfloat16),
            pltpu.SemaphoreType.DMA((bricks, 2)),
            pltpu.SemaphoreType.DMA((bricks, 2)),
        ],
        compiler_params=pltpu.CompilerParams(vmem_limit_bytes=room),
        cost_estimate=pl.CostEstimate(flops=bricks * 400_000_000, bytes_accessed=1024, transcendentals=0),
        name="pack",
    )(place, *pieces)


def partial_kernel(place, *refs):
    groups, (weights, out, packed) = refs[:4], refs[4:]
    z, core = place[0], place[1]
    for group, ref in enumerate(groups):
        from_core = core if group < 2 else 1 - core
        for brick, shift in enumerate(LATE if group % 2 else EARLY):
            from_z = lax.rem(z + shift + 8, 8)
            start = pl.multiple_of((from_z * 2 + from_core) * CAP, CAP)
            packed[:, pl.ds(start, CAP), :] = ref[:, brick * CAP : (brick + 1) * CAP, :]
    for sector in range(PLANE):
        code = turn_code(jnp.dot(weights[sector], packed[sector], preferred_element_type=jnp.float32))
        out[sector] = code.astype(jnp.int16).reshape(2, STEPS * ROWS, DEPTH)


def partial_codes(place, groups, weights):
    return pl.pallas_call(
        partial_kernel,
        out_shape=jax.ShapeDtypeStruct((PLANE, 2, STEPS * ROWS, DEPTH), jnp.int16),
        in_specs=[SMEM] + [VMEM] * 5,
        out_specs=VMEM,
        scratch_shapes=[pltpu.VMEM((PLANE, SLOTS, DEPTH), jnp.bfloat16)],
        compiler_params=pltpu.CompilerParams(vmem_limit_bytes=20 * MIB),
        cost_estimate=pl.CostEstimate(flops=2 * 537_000_000, bytes_accessed=8 * 1024 * 1024, transcendentals=0),
        name="partial",
    )(place, *groups, weights)


def sum_kernel(parts, out):
    for half in range(2):
        total = parts[0, half].astype(jnp.int32)
        for source in range(1, PLANE):
            total = total + parts[source, half].astype(jnp.int32)
        out[:, half * DEPTH : (half + 1) * DEPTH] = total


def sum_codes(parts):
    return pl.pallas_call(
        sum_kernel,
        out_shape=jax.ShapeDtypeStruct((STEPS * ROWS, NZ), jnp.int32),
        in_specs=[VMEM],
        out_specs=VMEM,
        compiler_params=pltpu.CompilerParams(vmem_limit_bytes=12 * MIB),
        cost_estimate=pl.CostEstimate(flops=2_000_000, bytes_accessed=2_500_000, transcendentals=0),
        name="sums",
    )(parts)


def edge_codes(parts):
    code = parts.astype(jnp.int32).sum(0)
    code = jnp.concatenate([code[0], code[1]], 1)
    return (((code + 32768) & 65535) - 32768).astype(jnp.int16)


def z_ring(value, shift):
    return lax.ppermute(value, "z", [(i, (i + shift) % 8) for i in range(8)])


def swap_core(value):
    return lax.ppermute(value, "c", [(0, 1), (1, 0)])


def first_step(brick):
    return z_ring(brick, 1), z_ring(brick, -1)


def gather_and_pack(place, first, brick, before, after, field):
    whole = {0: brick, -1: before, 1: after}
    for step in range(2, 4):
        for way in (-1, 1):
            whole[way * step] = z_ring(whole[way * (step - 1)], -way)
    early = pack(place, [whole[shift] for shift in EARLY], len(EARLY), 56 * MIB)
    early, whole[-3], whole[3] = lax.optimization_barrier((early, whole[-3], whole[3]))
    mine_early, other_early = early
    whole[4], fields = lax.optimization_barrier((z_ring(whole[-3], 1), exchange_field(first, field)))
    other_early = swap_core(other_early)
    mine_late, other_late = pack(place, [whole[shift] for shift in LATE], len(LATE), 12 * MIB)
    other_late = swap_core(other_late)
    return (mine_early, mine_late, other_early, other_late), fields


def nothing_packed(place, first, brick, before, after, field):
    rows = [jnp.zeros((PLANE, len(group) * CAP, DEPTH), brick.dtype) for group in (EARLY, LATE)]
    edges = [jnp.zeros((2, count, DEPTH), field.dtype) for count in (SHARED, HALO)]
    return (rows[0], rows[1], rows[0], rows[1]), (edges[0], edges[1], edges[1])


def per_device(field, brick_speed, send_index, send_count, weights, propagator):
    slots = lax.broadcasted_iota(jnp.int32, send_index.shape, 2)
    chosen = jnp.where(slots < send_count[:, :, None], send_index, -1).astype(jnp.bfloat16)
    chosen = chosen.reshape(8, 8, 2, CAP).transpose(0, 2, 1, 3).reshape(16, BCOL)
    brick = jnp.concatenate([jnp.pad(chosen, ((0, 0), (0, DEPTH - BCOL))), brick_speed])
    place = jnp.stack([lax.axis_index("z"), lax.axis_index("c")]).astype(jnp.int32)
    side = lax.axis_index("yl").astype(jnp.int32).reshape(1)
    brick, place, side = lax.optimization_barrier((brick, place, side))
    first = side[0] == 0

    before, after = first_step(brick)
    before, after, moved = lax.optimization_barrier((before, after, sort_weights(weights)))
    moved = lax.all_to_all(moved, ("x", "yh"), split_axis=0, concat_axis=0, tiled=True)
    field = field.transpose(1, 0, 2)
    groups, (partner, near, far) = lax.cond(
        send_count[0, 0] <= CAP, gather_and_pack, nothing_packed, place, first, brick, before, after, field
    )
    parts = partial_codes(place, groups, moved)

    parts = lax.all_to_all(
        parts.reshape(2 * PLANE, STEPS * ROWS, DEPTH), ("x", "yh", "yl"), split_axis=0, concat_axis=0, tiled=True
    ).reshape(PLANE, 2, STEPS * ROWS, DEPTH)
    edge = STEPS * HALO
    edges = (edge_codes(parts[:, :, -edge:]), edge_codes(parts[:, :, :edge]))
    code_left, code_right = ring_step(edges[0], 1), ring_step(edges[1], -1)
    code = sum_codes(parts)

    keep, send = march(side, code, code_left, code_right, field, partner, near, far, propagator)
    return merge(side, keep, swap_dep(send))


def solution(mesh):
    inner = Mesh(mesh.devices.reshape(SIZES), AXES)
    placed = (
        P(SECTOR, None, "yl"),
        P(SECTOR, "yl"),
        P(SECTOR, None, None),
        P(SECTOR, None),
        P(SECTOR, None, None),
        P(),
    )
    return jax.shard_map(
        per_device, mesh=inner, in_specs=placed, out_specs=P(SECTOR, None, "yl"), check_vma=False
    )
```

```python
import math

import jax
import jax.numpy as jnp
from jax import lax
from jax.experimental import pallas as pl
from jax.experimental.pallas import tpu as pltpu
from jax.sharding import Mesh, PartitionSpec as P

angle_rate = 200.0 / 1500.0
couple_real = 0.1
couple_imag = 0.15

AXES = ("z", "x", "yh", "c", "yl")
SECTOR = ("z", "x", "yh", "c")
SIZES = (8, 4, 2, 2, 2)
HALO = 8
ROWS = 32
EXT = ROWS + 2 * HALO
SHARED = ROWS + HALO
NZ = 1024
DEPTH = NZ // 2
STEPS = 4
FACTORS = 2
RING = 256
MIB = 1024 * 1024
VMEM = pl.BlockSpec(memory_space=pltpu.VMEM)
SMEM = pl.BlockSpec(memory_space=pltpu.SMEM)
ANY = pl.BlockSpec(memory_space=pl.ANY)


def turn_code(speed):
    turns = speed * (-angle_rate / (2.0 * math.pi))
    code = jnp.round((turns - jnp.round(turns)) * 65536.0).astype(jnp.int32)
    return jnp.where(code > 32767, -32768, code)


def cos_sin(code):
    quadrant = (code + 8192) >> 14
    part = (code - (quadrant << 14)).astype(jnp.float32) * (1.0 / 16384.0)
    square = part * part
    h = math.pi / 2
    sine = part * (h + square * (-(h**3) / 6 + square * (h**5 / 120 - square * (h**7 / 5040))))
    cosine = 1.0 + square * (
        -(h**2) / 2 + square * (h**4 / 24 + square * (-(h**6) / 720 + square * (h**8 / 40320)))
    )
    odd = (quadrant & 1) == 1
    first = jnp.where(odd, sine, cosine)
    second = jnp.where(odd, cosine, sine)
    first = jnp.where(((quadrant + 1) & 2) == 2, -first, first)
    second = jnp.where((quadrant & 2) == 2, -second, second)
    return first, second


def march_kernel(side, code, code_left, code_right, field, partner, near, far, factors, keep, send, *scratch):
    state, padded, rounded, codes = scratch
    second = side[0]
    first = second == 0
    rows = pl.ds(pl.multiple_of(HALO * (1 - second), HALO), SHARED)
    outer = pl.ds(pl.multiple_of(SHARED * second, HALO), HALO)
    here = pl.ds(pl.multiple_of(DEPTH * second, DEPTH), DEPTH)
    there = pl.ds(pl.multiple_of(DEPTH * (1 - second), DEPTH), DEPTH)
    state[:, rows, here] = field[:, pl.ds(pl.multiple_of((2 * ROWS - SHARED) * second, HALO), SHARED)]
    state[:, rows, there] = partner[...]
    state[:, outer, here] = far[...]
    state[:, outer, there] = near[...]
    padded[:, 0:HALO] = jnp.zeros((2, HALO, NZ), jnp.float32)
    padded[:, HALO + EXT :] = jnp.zeros((2, HALO, NZ), jnp.float32)
    edge, body = STEPS * HALO, STEPS * ROWS
    for chunk in range(NZ // 128):
        lanes = slice(chunk * 128, (chunk + 1) * 128)
        codes[chunk, 0:edge] = code_left[:, lanes].astype(jnp.int32)
        codes[chunk, edge : edge + body] = ((code[:, lanes] + 32768) & 65535) - 32768
        codes[chunk, edge + body :] = code_right[:, lanes].astype(jnp.int32)
    for step in range(STEPS):
        for chunk in range(NZ // 128):
            lanes = slice(chunk * 128, (chunk + 1) * 128)
            cosine, sine = cos_sin(codes[chunk, pl.ds(step, EXT, stride=STEPS), :])
            real = state[0, :, lanes]
            imag = state[1, :, lanes]
            padded[0, HALO : HALO + EXT, lanes] = real * cosine - imag * sine
            padded[1, HALO : HALO + EXT, lanes] = real * sine + imag * cosine
        laplace = []
        for part in range(2):
            near = padded[part, HALO - 1 : HALO - 1 + EXT] + padded[part, HALO + 1 : HALO + 1 + EXT]
            far = padded[part, HALO - 2 : HALO - 2 + EXT] + padded[part, HALO + 2 : HALO + 2 + EXT]
            centre = padded[part, HALO : HALO + EXT]
            laplace.append((16.0 * near - far - 30.0 * centre) * (1.0 / 12.0))
        rounded[0:EXT] = (
            padded[0, HALO : HALO + EXT] + couple_real * laplace[0] - couple_imag * laplace[1]
        ).astype(jnp.bfloat16)
        rounded[EXT : 2 * EXT] = (
            padded[1, HALO : HALO + EXT] + couple_real * laplace[1] + couple_imag * laplace[0]
        ).astype(jnp.bfloat16)
        for factor in range(FACTORS):
            left = rounded[...]
            for column in range(0, NZ, 256):
                by_real = jnp.dot(
                    left, factors[factor, 0, :, column : column + 256], preferred_element_type=jnp.float32
                )
                by_imag = jnp.dot(
                    left, factors[factor, 1, :, column : column + 256], preferred_element_type=jnp.float32
                )
                state[0, :, column : column + 256] = by_real[:EXT] - by_imag[EXT:]
                state[1, :, column : column + 256] = by_imag[:EXT] + by_real[EXT:]
            if factor + 1 < FACTORS:
                rounded[0:EXT] = state[0].astype(jnp.bfloat16)
                rounded[EXT : 2 * EXT] = state[1].astype(jnp.bfloat16)
    low = state[:, HALO : HALO + ROWS, 0:DEPTH]
    high = state[:, HALO : HALO + ROWS, DEPTH:NZ]
    keep[...] = jnp.where(first, low, high)
    send[...] = jnp.where(first, high, low).astype(jnp.bfloat16)


def march(side, code, code_left, code_right, field, partner, near, far, factors):
    return pl.pallas_call(
        march_kernel,
        out_shape=(
            jax.ShapeDtypeStruct((2, ROWS, DEPTH), jnp.float32),
            jax.ShapeDtypeStruct((2, ROWS, DEPTH), jnp.bfloat16),
        ),
        in_specs=[SMEM] + [VMEM] * 8,
        out_specs=(VMEM, VMEM),
        scratch_shapes=[
            pltpu.VMEM((2, EXT, NZ), jnp.float32),
            pltpu.VMEM((2, EXT + 2 * HALO, NZ), jnp.float32),
            pltpu.VMEM((2 * EXT, NZ), jnp.bfloat16),
            pltpu.VMEM((NZ // 128, STEPS * EXT, 128), jnp.int32),
        ],
        compiler_params=pltpu.CompilerParams(vmem_limit_bytes=24 * MIB),
        cost_estimate=pl.CostEstimate(
            flops=2 * 8 * 2 * EXT * NZ * 2 * NZ, bytes_accessed=10 * 1024 * 1024, transcendentals=0
        ),
        name="march",
    )(side, code, code_left, code_right, field, partner, near, far, factors)


def merge_kernel(side, keep, other, out):
    for part in range(2):
        out[pl.ds(side[0] * ROWS, ROWS), part, :] = keep[part]
        out[pl.ds((1 - side[0]) * ROWS, ROWS), part, :] = other[part].astype(jnp.float32)


def merge(side, keep, other):
    return pl.pallas_call(
        merge_kernel,
        out_shape=jax.ShapeDtypeStruct((2 * ROWS, 2, DEPTH), jnp.float32),
        in_specs=[SMEM, VMEM, VMEM],
        out_specs=VMEM,
        compiler_params=pltpu.CompilerParams(vmem_limit_bytes=12 * MIB),
        name="merge",
    )(side, keep, other)


def swap_dep(value):
    return lax.ppermute(value, "yl", [(0, 1), (1, 0)])


def ring_step(value, shift):
    return lax.ppermute(value, AXES, [(i, (i + shift) % RING) for i in range(RING)])


def exchange_field(first, field):
    top, bottom = field[:, :HALO], field[:, -HALO:]
    partner = swap_dep(jnp.where(first, field[:, -SHARED:], field[:, :SHARED]))
    across = [(i, i + 1 if i % 2 else i - 1) for i in range(RING)]
    near = lax.ppermute(jnp.where(first, top, bottom), AXES, [(i, j % RING) for i, j in across])
    along = [(i, i - 2 if i % 2 else i + 2) for i in range(RING)]
    far = lax.ppermute(jnp.where(first, bottom, top), AXES, [(i, j % RING) for i, j in along])
    return partner, near, far


PLANE = 8
SLOTS = 512
BCOL = 256
CAP = 32
EARLY = (0, -1, 1, -2, 2)
LATE = (-3, 3, 4)


def sort_kernel(weights, out):
    rows = weights.shape[0] * STEPS
    lane = lax.broadcasted_iota(jnp.int32, (rows, 128), 1)
    for pair in range(4):
        for x in range(4):
            both = []
            for z in (2 * pair, 2 * pair + 1):
                start = z * SLOTS + x * 128
                both.append(weights[:, :, start : start + 128].astype(jnp.float32).reshape(rows, 128))
            even, odd = both
            out[2 * x, :, pair * 128 : pair * 128 + 128] = jnp.where(
                lane < 64, even, pltpu.roll(odd, 64, 1)
            ).astype(jnp.bfloat16)
            out[2 * x + 1, :, pair * 128 : pair * 128 + 128] = jnp.where(
                lane < 64, pltpu.roll(even, 64, 1), odd
            ).astype(jnp.bfloat16)


def sort_weights(weights):
    block = 16
    return pl.pallas_call(
        sort_kernel,
        out_shape=jax.ShapeDtypeStruct((PLANE, 2 * ROWS * STEPS, SLOTS), jnp.bfloat16),
        grid=(2 * ROWS // block,),
        in_specs=[pl.BlockSpec((block, STEPS, 8 * SLOTS), lambda i: (i, 0, 0))],
        out_specs=pl.BlockSpec((PLANE, block * STEPS, SLOTS), lambda i: (0, i, 0)),
        compiler_params=pltpu.CompilerParams(vmem_limit_bytes=12 * MIB),
        cost_estimate=pl.CostEstimate(flops=0, bytes_accessed=4 * 1024 * 1024, transcendentals=0),
        name="sort",
    )(weights)


def pack_kernel(place, *refs):
    bricks, outs = refs[:-2], refs[-2:]
    z, core = place[0], place[1]
    line = lax.broadcasted_iota(jnp.int32, (16, BCOL), 0)
    column = lax.broadcasted_iota(jnp.int32, (BCOL // 2, 2 * BCOL), 0)
    for brick, held in enumerate(bricks):
        table = held[0:16, 0:BCOL].astype(jnp.float32)
        index = jnp.concatenate(
            [
                jnp.sum(jnp.where(line == z * 2 + target, table, 0.0), axis=0, keepdims=True)
                for target in (core, 1 - core)
            ],
            axis=1,
        ).astype(jnp.int32)
        total = None
        for half in range(2):
            onehot = jnp.where(column + half * (BCOL // 2) == index, 1.0, 0.0).astype(jnp.bfloat16)
            start = 16 + half * (BCOL // 2)
            part = lax.dot_general(
                onehot, held[start : start + BCOL // 2, :], (((0,), (0,)), ((), ())), preferred_element_type=jnp.float32
            )
            total = part if total is None else total + part
        total = total.astype(jnp.bfloat16)
        for target, out in enumerate(outs):
            rows = total[target * BCOL : (target + 1) * BCOL].reshape(PLANE, CAP, DEPTH)
            out[:, brick * CAP : (brick + 1) * CAP, :] = rows


def pack(place, bricks):
    shape = jax.ShapeDtypeStruct((PLANE, len(bricks) * CAP, DEPTH), jnp.bfloat16)
    return pl.pallas_call(
        pack_kernel,
        out_shape=(shape, shape),
        in_specs=[SMEM] + [VMEM] * len(bricks),
        out_specs=(VMEM, VMEM),
        compiler_params=pltpu.CompilerParams(vmem_limit_bytes=12 * MIB),
        cost_estimate=pl.CostEstimate(flops=len(bricks) * 400_000_000, bytes_accessed=1024, transcendentals=0),
        name="pack",
    )(place, *bricks)


def partial_kernel(place, *refs):
    groups, (weights, out, packed) = refs[:4], refs[4:]
    z, core = place[0], place[1]
    for group, ref in enumerate(groups):
        from_core = core if group < 2 else 1 - core
        for brick, shift in enumerate(LATE if group % 2 else EARLY):
            from_z = lax.rem(z + shift + 8, 8)
            start = pl.multiple_of((from_z * 2 + from_core) * CAP, CAP)
            packed[:, pl.ds(start, CAP), :] = ref[:, brick * CAP : (brick + 1) * CAP, :]
    for sector in range(PLANE):
        code = turn_code(jnp.dot(weights[sector], packed[sector], preferred_element_type=jnp.float32))
        out[sector] = code.astype(jnp.int16).reshape(2, STEPS * ROWS, DEPTH)


def partial_codes(place, groups, weights):
    return pl.pallas_call(
        partial_kernel,
        out_shape=jax.ShapeDtypeStruct((PLANE, 2, STEPS * ROWS, DEPTH), jnp.int16),
        in_specs=[SMEM] + [VMEM] * 5,
        out_specs=VMEM,
        scratch_shapes=[pltpu.VMEM((PLANE, SLOTS, DEPTH), jnp.bfloat16)],
        compiler_params=pltpu.CompilerParams(vmem_limit_bytes=20 * MIB),
        cost_estimate=pl.CostEstimate(flops=2 * 537_000_000, bytes_accessed=8 * 1024 * 1024, transcendentals=0),
        name="partial",
    )(place, *groups, weights)


def sum_kernel(parts, out):
    for half in range(2):
        total = parts[0, half].astype(jnp.int32)
        for source in range(1, PLANE):
            total = total + parts[source, half].astype(jnp.int32)
        out[:, half * DEPTH : (half + 1) * DEPTH] = total


def sum_codes(parts):
    return pl.pallas_call(
        sum_kernel,
        out_shape=jax.ShapeDtypeStruct((STEPS * ROWS, NZ), jnp.int32),
        in_specs=[VMEM],
        out_specs=VMEM,
        compiler_params=pltpu.CompilerParams(vmem_limit_bytes=12 * MIB),
        cost_estimate=pl.CostEstimate(flops=2_000_000, bytes_accessed=2_500_000, transcendentals=0),
        name="sums",
    )(parts)


def edge_codes(parts):
    code = parts.astype(jnp.int32).sum(0)
    code = jnp.concatenate([code[0], code[1]], 1)
    return (((code + 32768) & 65535) - 32768).astype(jnp.int16)


def z_ring(value, shift):
    return lax.ppermute(value, "z", [(i, (i + shift) % 8) for i in range(8)])


def swap_core(value):
    return lax.ppermute(value, "c", [(0, 1), (1, 0)])


def first_step(brick):
    return z_ring(brick, 1), z_ring(brick, -1)


def gather_and_pack(place, first, brick, before, after, field):
    whole = {0: brick, -1: before, 1: after}
    for step in range(2, 4):
        for way in (-1, 1):
            whole[way * step] = z_ring(whole[way * (step - 1)], -way)
    early = pack(place, [whole[shift] for shift in EARLY])
    early, whole[-3], whole[3] = lax.optimization_barrier((early, whole[-3], whole[3]))
    mine_early, other_early = early
    whole[4], fields = lax.optimization_barrier((z_ring(whole[-3], 1), exchange_field(first, field)))
    other_early = swap_core(other_early)
    mine_late, other_late = pack(place, [whole[shift] for shift in LATE])
    other_late = swap_core(other_late)
    return (mine_early, mine_late, other_early, other_late), fields


def nothing_packed(place, first, brick, before, after, field):
    rows = [jnp.zeros((PLANE, len(group) * CAP, DEPTH), brick.dtype) for group in (EARLY, LATE)]
    edges = [jnp.zeros((2, count, DEPTH), field.dtype) for count in (SHARED, HALO)]
    return (rows[0], rows[1], rows[0], rows[1]), (edges[0], edges[1], edges[1])


def per_device(field, brick_speed, send_index, send_count, weights, propagator):
    slots = lax.broadcasted_iota(jnp.int32, send_index.shape, 2)
    chosen = jnp.where(slots < send_count[:, :, None], send_index, -1).astype(jnp.bfloat16)
    chosen = chosen.reshape(8, 8, 2, CAP).transpose(0, 2, 1, 3).reshape(16, BCOL)
    brick = jnp.concatenate([jnp.pad(chosen, ((0, 0), (0, DEPTH - BCOL))), brick_speed])
    place = jnp.stack([lax.axis_index("z"), lax.axis_index("c")]).astype(jnp.int32)
    side = lax.axis_index("yl").astype(jnp.int32).reshape(1)
    brick, place, side = lax.optimization_barrier((brick, place, side))
    first = side[0] == 0

    before, after = first_step(brick)
    before, after, moved = lax.optimization_barrier((before, after, sort_weights(weights)))
    moved = lax.all_to_all(moved, ("x", "yh"), split_axis=0, concat_axis=0, tiled=True)
    field = field.transpose(1, 0, 2)
    groups, (partner, near, far) = lax.cond(
        send_count[0, 0] <= CAP, gather_and_pack, nothing_packed, place, first, brick, before, after, field
    )
    parts = partial_codes(place, groups, moved)

    parts = lax.all_to_all(
        parts.reshape(2 * PLANE, STEPS * ROWS, DEPTH), ("x", "yh", "yl"), split_axis=0, concat_axis=0, tiled=True
    ).reshape(PLANE, 2, STEPS * ROWS, DEPTH)
    edge = STEPS * HALO
    edges = (edge_codes(parts[:, :, -edge:]), edge_codes(parts[:, :, :edge]))
    code_left, code_right = ring_step(edges[0], 1), ring_step(edges[1], -1)
    code = sum_codes(parts)

    keep, send = march(side, code, code_left, code_right, field, partner, near, far, propagator)
    return merge(side, keep, swap_dep(send))


def solution(mesh):
    inner = Mesh(mesh.devices.reshape(SIZES), AXES)
    placed = (
        P(SECTOR, None, "yl"),
        P(SECTOR, "yl"),
        P(SECTOR, None, None),
        P(SECTOR, None),
        P(SECTOR, None, None),
        P(),
    )
    return jax.shard_map(
        per_device, mesh=inner, in_specs=placed, out_specs=P(SECTOR, None, "yl"), check_vma=False
    )
```
